128 devices in a mesh: seg: 8 (over x, core), sec: 16 (over z, y).
Axes of the slice: x: 4, y: 4, z: 4, core: 2. Of those that a mesh axis runs over, the one named last changes fastest.
Arguments:
- psi: bfloat16 [8, 48, 128, 128], P('seg', 'sec'), may hold values from -600 to 600
- env_left: bfloat16 [8, 48, 40, 128, 128], P('seg', 'sec'), may hold values from -0.5 to 0.5
- env_right: bfloat16 [8, 48, 40, 128, 128], P('seg', 'sec'), may hold values from -0.5 to 0.5
- site_left: bfloat16 [8, 48, 128, 128], P('seg', 'sec'), may hold values from -0.5 to 0.5
- site_right: bfloat16 [8, 48, 128, 128], P('seg', 'sec'), may hold values from -0.5 to 0.5
- mix_left: float32 [8, 40, 40], P('seg'), may hold values from -1 to 1
- mix_right: float32 [8, 40, 40], P('seg'), may hold values from -1 to 1
- sources: int32 [8, 48, 6], P('seg', 'sec'), may hold values from 0 to 47
- terms: int32 [8, 48, 6], P('seg', 'sec'), may hold values from 0 to 7
- term_coef: float32 [8, 40], replicated, may hold values from -0.375 to 0.375
- energy: float32 [8, 48, 128], P('seg', 'sec'), may hold values from 0.5 to 4
Outputs:
- lanczos_vector: bfloat16 [8, 48, 128, 128], P('seg', 'sec')
- next_residual: float32 [8, 48, 128, 128], P('seg', 'sec')
- coefficients: float32 [8, 11], P('seg')
The draws below stay inside these ranges and needn't reach their ends.
All inputs are finite; a program needn't handle non-finite values.
Results may differ from the reference program's by a relative error of at most 0.015.
Values may be sent and summed in bfloat16 or wider, within the bound.
A program may use at most 128 MiB of HBM per device.

```python
import math
import jax
import jax.numpy as jnp
from jax import lax

W = 40
BD = 128
ENT = 6
TERMS = 8
APPS = 6
BLK_DEV = 3
BLOCKS = 48
SEGS = 8


def draw_psi(key, part):
    key = jax.random.fold_in(key, 11)
    first, second = jax.random.split(key, 2)
    ramp = 1.0 + 2.0 * jnp.arange(BLOCKS, dtype=jnp.float32) / (BLOCKS - 1)
    rows = jnp.exp(jax.random.uniform(second, (SEGS, BLOCKS, BD, 1), minval=0.0, maxval=math.log(10.0)))
    base = jnp.clip(jax.random.normal(first, (SEGS, BLOCKS, BD, BD)), -4.0, 4.0)
    values = base * rows * ramp[None, :, None, None]
    return values.astype(jnp.bfloat16)


def draw_energy(key, part):
    key = jax.random.fold_in(key, 23)
    first, second, third = jax.random.split(key, 3)
    owners = BLOCKS // BLK_DEV
    shard_level = jax.random.uniform(first, (SEGS, owners, 1), minval=0.0, maxval=1.0)
    shard_level = jnp.repeat(shard_level, BLK_DEV, axis=1)
    block_level = jax.random.uniform(second, (SEGS, BLOCKS, 1), minval=0.0, maxval=1.0)
    state_level = jax.random.uniform(third, (SEGS, BLOCKS, BD), minval=0.0, maxval=1.0)
    mixed = 0.55 * shard_level + 0.1 * block_level + 0.35 * state_level
    values = 0.5 * jnp.exp(math.log(8.0) * mixed)
    return values.astype(jnp.float32)


def set_ends(values, stream_key, smallest, high):
    dims = values.shape
    place = [jax.random.randint(jax.random.fold_in(stream_key, axis), (), 0, dims[axis]) for axis in range(len(dims))]
    values = values.at[tuple(place)].set(smallest)
    longest = dims.index(max(dims))
    place[longest] = (place[longest] + 1) % dims[longest]
    return values.at[tuple(place)].set(high)


def shard_levels(rng, shape, cuts, smallest, high):
    gain = 1.0
    for position, blocks in cuts:
        draws = jax.random.uniform(jax.random.fold_in(jax.random.fold_in(rng, 6), position), (blocks,), jnp.float32, smallest / len(cuts), high / len(cuts))
        gain = gain * jnp.repeat(jnp.exp(draws), shape[position] // blocks).reshape((-1,) + (1,) * (len(shape) - 1 - position))
    return gain


def bell_draw(rng, dims, spread, most, cuts=(), held_as=jnp.bfloat16):
    drawn = spread * jax.random.normal(rng, dims, jnp.float32)
    if cuts:
        drawn = drawn * shard_levels(rng, dims, cuts, -0.22, 0.18)
    return jnp.clip(drawn, -most, most).astype(held_as)


def setup_inputs(seed: int = 0) -> dict:
    streams_of = jax.random.split(jax.random.key(seed), 12)
    return {
        "psi": draw_psi(jax.random.fold_in(streams_of[11], 71), 0),
        "env_left": bell_draw(streams_of[1], (SEGS, BLOCKS, W, BD, BD), BD ** -0.5, 0.5, ((0, 8), (1, 16))),
        "env_right": bell_draw(streams_of[2], (SEGS, BLOCKS, W, BD, BD), BD ** -0.5, 0.5, ((0, 8), (1, 16))),
        "site_left": bell_draw(streams_of[3], (SEGS, BLOCKS, BD, BD), BD ** -0.5, 0.5, ((0, 8), (1, 16))),
        "site_right": bell_draw(streams_of[4], (SEGS, BLOCKS, BD, BD), BD ** -0.5, 0.5, ((0, 8), (1, 16))),
        "mix_left": bell_draw(streams_of[5], (SEGS, W, W), W ** -0.5, 1.0, ((0, 8),), jnp.float32),
        "mix_right": bell_draw(streams_of[6], (SEGS, W, W), W ** -0.5, 1.0, ((0, 8),), jnp.float32),
        "sources": set_ends(jax.random.randint(streams_of[7], (SEGS, BLOCKS, ENT), 0, BLOCKS), jax.random.fold_in(streams_of[7], 1), 0, BLOCKS - 1).astype(jnp.int32),
        "terms": set_ends(jax.random.randint(streams_of[8], (SEGS, BLOCKS, ENT), 0, TERMS), jax.random.fold_in(streams_of[8], 1), 0, TERMS - 1).astype(jnp.int32),
        "term_coef": bell_draw(streams_of[9], (TERMS, W), (W * ENT) ** -0.5, 0.375, (), jnp.float32),
        "energy": draw_energy(jax.random.fold_in(streams_of[11], 71), 0),
    }


EPSILON = 1e-06
HIGH = lax.Precision.HIGHEST

def grow(env, site, mix):
    mixed = jnp.einsum('vw,bwij->bvij', mix, env.astype(jnp.float32), precision=HIGH).astype(jnp.bfloat16)
    half = jnp.einsum('bvij,bjk->bvik', mixed.astype(jnp.float32), site.astype(jnp.float32)).astype(jnp.bfloat16)
    return jnp.einsum('bji,bvjk->bvik', site.astype(jnp.float32), half.astype(jnp.float32)).astype(jnp.bfloat16)

def apply_operator(vector, left_env, right_env, weights, sources, energy):
    picked = vector[sources].astype(jnp.float32)
    combo = jnp.einsum('tkw,tkij->twij', weights, picked, precision=HIGH).astype(jnp.bfloat16)
    inner = jnp.einsum('twij,twjk->twik', left_env.astype(jnp.float32), combo.astype(jnp.float32)).astype(jnp.bfloat16)
    image = jnp.einsum('twik,twlk->til', inner.astype(jnp.float32), right_env.astype(jnp.float32))
    return image + energy[:, :, None] * vector.astype(jnp.float32)

def lanczos(vector, left_env, right_env, weights, sources, energy):
    count = float(vector.shape[0] * vector.shape[1] * vector.shape[2])
    start = vector.astype(jnp.float32)
    norm0 = jnp.sqrt(jnp.sum(start * start) / count + EPSILON)
    first_vector = start / norm0
    image = apply_operator(vector, left_env, right_env, weights, sources, energy) / norm0
    alpha0 = jnp.sum(first_vector * image) / count
    rest = image - alpha0 * first_vector
    beta = jnp.sqrt(jnp.sum(rest * rest) / count + EPSILON)
    coefs = [alpha0, beta]
    previous = first_vector
    current = (rest / beta).astype(jnp.bfloat16)
    for step in range(1, APPS):
        image = apply_operator(current, left_env, right_env, weights, sources, energy)
        current_f = current.astype(jnp.float32)
        alpha = jnp.sum(current_f * image) / count
        rest = image - alpha * current_f - beta * previous
        coefs.append(alpha)
        if step < APPS - 1:
            beta = jnp.sqrt(jnp.sum(rest * rest) / count + EPSILON)
            coefs.append(beta)
            previous = current_f
            current = (rest / beta).astype(jnp.bfloat16)
    return (current, rest, jnp.stack(coefs))

def reference(psi, env_left, env_right, site_left, site_right, mix_left, mix_right, sources, terms, term_coef, energy):

    def one_segment(index):
        before = jnp.maximum(index - 1, 0)
        after = jnp.minimum(index + 1, SEGS - 1)
        grown_l = grow(env_left[before], site_left[before], mix_left[before])
        grown_r = grow(env_right[after], site_right[after], mix_right[after])
        left_env = jnp.where(index == 0, env_left[index], grown_l)
        right_env = jnp.where(index == SEGS - 1, env_right[index], grown_r)
        weights = term_coef[terms[index]]
        return lanczos(psi[index], left_env, right_env, weights, sources[index], energy[index])
    return lax.map(one_segment, jnp.arange(SEGS, dtype=jnp.int32))
```

```python
import functools

import jax
import jax.numpy as jnp
from jax import lax
from jax.experimental import pallas as pl
from jax.experimental.pallas import tpu as pltpu
from jax.sharding import PartitionSpec as P

APPS = 6
EPSILON = 1e-06
CH = 40
BD = 128
ENT = 6
BLK = 3
HALF = BD // 2
TILE = 16
MESH = pl.DeviceIdType.MESH
BF = jnp.bfloat16
F32 = jnp.float32

CHUNK = 8
CHUNKS = CH // CHUNK
GROUPS = ((0, 3),)


def dot(a, b):
    return lax.dot_general(a, b, (((1,), (0,)), ((), ())), preferred_element_type=F32)


def dot_nt(a, b):
    return lax.dot_general(a, b, (((1,), (1,)), ((), ())), preferred_element_type=F32)


def total(x):
    lanes = jnp.sum(x, axis=0, keepdims=True)
    return jnp.broadcast_to(jnp.sum(lanes, axis=1, keepdims=True), (1, BD))


def split(x):
    high = x.astype(BF)
    return high, (x - high.astype(F32)).astype(BF)


def wait_bytes(ref, sem):
    pltpu.make_async_copy(ref, ref, sem).wait()


def spread(rows, start):
    row = lax.broadcasted_iota(jnp.int32, (rows, CH), 0) + start
    return (row // TILE == lax.broadcasted_iota(jnp.int32, (rows, CH), 1)).astype(BF)


def same_state(rows, cols):
    row = lax.broadcasted_iota(jnp.int32, (rows, cols), 0)
    col = lax.broadcasted_iota(jnp.int32, (rows, cols), 1)
    return row % TILE == col % TILE


def kernel(
    segs,
    count,
    psi,
    env_left,
    env_right,
    site_left,
    site_right,
    mix_left,
    mix_right,
    sources,
    terms,
    term_coef,
    energy,
    out_vector,
    out_rest,
    out_coef,
    env_in,
    grown,
    envs,
    mixed,
    mix_kron,
    site_t,
    term_kron,
    combo,
    image,
    on_site,
    picked,
    own,
    before,
    leftover,
    half0,
    half1,
    stats,
    local0,
    local1,
    local_stats,
    place,
    load_sem,
    env_send,
    env_recv,
    s1,
    r1,
    s2,
    r2,
    stat_send,
    stat_recv,
):
    seg = lax.axis_index("seg")
    sec = lax.axis_index("sec")
    my_z = sec // 4
    my_y = sec % 4

    def along_z(d):
        return (seg, ((my_z + d) % 4) * 4 + my_y)

    def along_y(d):
        return (seg, my_z * 4 + (my_y + d) % 4)

    def send(src, dst, ssem, rsem, device):
        pltpu.make_async_remote_copy(
            src_ref=src, dst_ref=dst, send_sem=ssem, recv_sem=rsem,
            device_id=device, device_id_type=MESH,
        ).start()

    loads = []
    for b in range(BLK):
        for side, ref in ((0, env_left), (1, env_right)):
            c = pltpu.make_async_copy(ref.at[b], env_in.at[side, b], load_sem.at[side, b])
            c.start()
            loads.append(c)

    barrier = pltpu.get_barrier_semaphore()
    for d in (1, 2, 3):
        pl.semaphore_signal(barrier, inc=1, device_id=along_z(d), device_id_type=MESH)
        pl.semaphore_signal(barrier, inc=1, device_id=along_y(d), device_id_type=MESH)

    @pl.when(seg > 0)
    def _():
        pl.semaphore_signal(barrier, inc=1, device_id=(seg - 1, sec), device_id_type=MESH)

    @pl.when(seg < segs - 1)
    def _():
        pl.semaphore_signal(barrier, inc=1, device_id=(seg + 1, sec), device_id_type=MESH)

    def end_copy(side):
        source = env_left if side == 0 else env_right
        return pltpu.make_async_copy(source, envs.at[side], load_sem.at[side, BLK])

    @pl.when(seg == 0)
    def _():
        end_copy(0).start()

    @pl.when(seg == segs - 1)
    def _():
        end_copy(1).start()

    for side, ref in ((0, mix_left), (1, mix_right)):
        for part, mix in enumerate(split(ref[...])):
            def build(m, _, side=side, part=part, mix=mix):
                rows = dot(spread(BD, m * BD), mix).astype(BF)
                full = dot_nt(rows, spread(CH * TILE, 0))
                keep = same_state(BD, CH * TILE)
                at = pl.ds(pl.multiple_of(m * BD, BD), BD)
                mix_kron[side, part, at, :] = jnp.where(keep, full, 0.0).astype(BF)
                return 0

            lax.fori_loop(0, CH * TILE // BD, build, 0)

    eye_row = lax.broadcasted_iota(jnp.int32, (BD, BD), 0)
    eye = (eye_row == lax.broadcasted_iota(jnp.int32, (BD, BD), 1)).astype(BF)
    for side, ref in ((0, site_left), (1, site_right)):
        for b in range(BLK):
            site_t[side, b] = dot_nt(eye, ref[b]).astype(BF)

    for p in range(2):
        stats[p, 0, 0] = jnp.zeros((2, 8, BD), F32)
    for t in range(BLK):
        half0[0, t, 0, 0] = psi[t, :HALF, :]
        half1[0, t, 0, 0] = psi[t, HALF:, :]
        own[t] = psi[t]

    pl.semaphore_wait(
        barrier, 6 + jnp.where(seg > 0, 1, 0) + jnp.where(seg < segs - 1, 1, 0)
    )

    def gather_first(p, g):
        ts = pl.ds(*GROUPS[g])
        for d in (1, 3, 2):
            back = (4 - d) % 4
            send(half0.at[p, ts, 0, 0], half0.at[p, ts, 0, back], s1.at[p, g, 0], r1.at[p, g, 0], along_z(d))
            send(half1.at[p, ts, 0, 0], half1.at[p, ts, 0, back], s1.at[p, g, 1], r1.at[p, g, 1], along_y(d))

    def gather_second(p, g):
        ts = pl.ds(*GROUPS[g])
        for h, ref, along in ((0, half0, along_y), (1, half1, along_z)):
            wait_bytes(ref.at[p, ts, 0, pl.ds(1, 3)], r1.at[p, g, h])
            for d in (1, 3, 2):
                back = (4 - d) % 4
                send(ref.at[p, ts, 0], ref.at[p, ts, back], s2.at[p, g, h], r2.at[p, g, h], along(d))

    def gather_end(p):
        for g, group in enumerate(GROUPS):
            ts = pl.ds(*group)
            for h, ref in ((0, half0), (1, half1)):
                wait_bytes(ref.at[p, ts, pl.ds(1, 3)], r2.at[p, g, h])
                wait_bytes(ref.at[p, ts, 0, pl.ds(1, 3)], s1.at[p, g, h])
                wait_bytes(ref.at[p, ts, pl.ds(1, 3)], s2.at[p, g, h])

    def stats_first(p):
        for d in (1, 3, 2):
            send(stats.at[p, 0, 0], stats.at[p, 0, (4 - d) % 4], stat_send.at[p, 0], stat_recv.at[p, 0], along_z(d))

    def stats_second(p):
        wait_bytes(stats.at[p, 0, pl.ds(1, 3)], stat_recv.at[p, 0])
        for d in (1, 3, 2):
            send(stats.at[p, 0], stats.at[p, (4 - d) % 4], stat_send.at[p, 1], stat_recv.at[p, 1], along_y(d))

    def stats_end(p):
        wait_bytes(stats.at[p, pl.ds(1, 3)], stat_recv.at[p, 1])
        wait_bytes(stats.at[p, 0, pl.ds(1, 3)], stat_send.at[p, 0])
        wait_bytes(stats.at[p, pl.ds(1, 3)], stat_send.at[p, 1])

    for g in range(len(GROUPS)):
        gather_first(0, g)

    def env_copy(side, b, c):
        part = pl.ds(c * CHUNK, CHUNK)
        to = seg + 1 if side == 0 else seg - 1
        return pltpu.make_async_remote_copy(
            src_ref=grown.at[side, b, part],
            dst_ref=envs.at[side, b, part],
            send_sem=env_send.at[side, b, c],
            recv_sem=env_recv.at[side, b, c],
            device_id=(to, sec),
            device_id_type=MESH,
        )

    def grow(step, _):
        b = step // CHUNKS
        c = step % CHUNKS
        for side, site in ((0, site_left), (1, site_right)):
            @pl.when(c == 0)
            def _(side=side):
                wait_bytes(env_in.at[side, b], load_sem.at[side, b])

            rows = pl.ds(pl.multiple_of(c * CHUNK * TILE, CHUNK * TILE), CHUNK * TILE)
            high = mix_kron[side, 0, rows, :]
            low = mix_kron[side, 1, rows, :]
            for i in range(BD // (2 * TILE)):
                base = i * 2 * TILE
                cols = [
                    env_in[side, b, :, base + h * TILE:base + (h + 1) * TILE, :].reshape(CH * TILE, BD)
                    for h in range(2)
                ]
                both = jnp.concatenate(cols, axis=1)
                out = (dot(high, both) + dot(low, both)).astype(BF)
                for h in range(2):
                    mixed[:, base + h * TILE:base + (h + 1) * TILE, :] = out[:, h * BD:(h + 1) * BD].reshape(
                        CHUNK, TILE, BD
                    )
            half = dot(mixed[...].reshape(CHUNK * BD, BD), site[b]).astype(BF)
            wide = jnp.concatenate([half[v * BD:(v + 1) * BD] for v in range(CHUNK)], axis=1)
            done = dot(site_t[side, b], wide).astype(BF)
            for v in range(CHUNK):
                grown[side, b, c * CHUNK + v] = done[:, v * BD:(v + 1) * BD]

            @pl.when(seg < segs - 1 if side == 0 else seg > 0)
            def _(side=side):
                env_copy(side, b, c).start()

        return 0

    lax.fori_loop(0, BLK * CHUNKS, grow, 0)

    for g in range(len(GROUPS)):
        gather_second(0, g)

    for t in range(BLK):
        row = jnp.broadcast_to(energy[t:t + 1, :], (BD, BD))
        on_site[t] = jnp.transpose(row)
    spread_all = spread(CH * TILE, 0)
    keep = same_state(CH * TILE, ENT * TILE)
    for t in range(BLK):
        entry = lax.broadcasted_iota(jnp.int32, (8, ENT * TILE), 1) // TILE
        kind = jnp.zeros((8, ENT * TILE), jnp.int32)
        for k in range(ENT):
            kind = jnp.where(entry == k, terms[t, k], kind)
        hit = (kind == lax.broadcasted_iota(jnp.int32, (8, ENT * TILE), 0)).astype(BF)
        for part, coef in enumerate(split(term_coef[...])):
            rows = dot_nt(spread_all, coef).astype(BF)
            full = dot(rows, hit)
            term_kron[t, :, part * ENT * TILE:(part + 1) * ENT * TILE] = jnp.where(keep, full, 0.0).astype(BF)

    def where_is(t, k):
        s = sources[t, k]
        owner = s // BLK
        sub = s - BLK * owner
        return sub, (owner % 4 - my_y + 4) % 4, (owner // 4 - my_z + 4) % 4

    for t in range(BLK):
        for k in range(ENT):
            for n, value in enumerate(where_is(t, k)):
                place[n, t * ENT + k] = value

    gather_end(0)

    local0[...] = half0[0]
    local1[...] = half1[0]

    def fetch(q, _):
        sub, y, z = place[0, q], place[1, q], place[2, q]
        picked[q, :HALF, :] = local0[sub, y, z]
        picked[q, HALF:, :] = local1[sub, z, y]
        return 0

    lax.fori_loop(0, BLK * ENT, fetch, 0)

    def squares(n, acc):
        t, o = n // 4, n % 4
        for i in range(4):
            for ref in (half0, half1):
                x = ref[0, t, o, i].astype(F32)
                acc = acc + x * x
        return acc

    norm = total(lax.fori_loop(0, BLK * 4, squares, jnp.zeros((HALF, BD), F32)))
    sigma0 = 1.0 / jnp.sqrt(norm / count + EPSILON)

    def combine(t):
        for i in range(BD // (2 * TILE)):
            base = i * 2 * TILE
            cols = [
                picked[t * ENT:(t + 1) * ENT, base + h * TILE:base + (h + 1) * TILE, :].reshape(ENT * TILE, BD)
                for h in range(2)
            ]
            both = jnp.concatenate(cols, axis=1)
            out = dot(term_kron[t], jnp.concatenate([both, both], axis=0)).astype(BF)
            for h in range(2):
                combo[t, :, base + h * TILE:base + (h + 1) * TILE, :] = out[:, h * BD:(h + 1) * BD].reshape(
                    CH, TILE, BD
                )

    def contract(t, first, n):
        inner = [dot(envs[0, t, first + j], combo[t, first + j]).astype(BF) for j in range(n)]
        right = [envs[1, t, first + j] for j in range(n)]
        return dot_nt(jnp.concatenate(inner, axis=1), jnp.concatenate(right, axis=1))

    def finish(p, t, applied, sigma, beta):
        v = own[t].astype(F32) * sigma
        img = applied * sigma + on_site[t] * v
        w = img if beta is None else img - beta * before[t]
        prod = total(img * v)
        norm = total(v * v)
        over = total(w * v)
        a = jnp.where(norm > 0.0, over / jnp.where(norm > 0.0, norm, 1.0), 0.0)
        y = w - a * v
        leftover[t] = y
        low = y.astype(BF)
        half0[p, t, 0, 0] = low[:HALF]
        half1[p, t, 0, 0] = low[HALF:]
        stats[p, 0, 0, 0, t:t + 1, :] = prod
        stats[p, 0, 0, 0, 4 + t:5 + t, :] = norm
        stats[p, 0, 0, 1, t:t + 1, :] = a
        stats[p, 0, 0, 1, 4 + t:5 + t, :] = total(y * y)

    def scalars(p):
        def add(x):
            lines = jnp.sum(x.reshape(16, 4, BD), axis=0)
            return jnp.sum(lines, axis=0, keepdims=True)

        alpha = add(stats[p, :, :, 0, 0:4, :]) / count
        gap = alpha - stats[p, :, :, 1, 0:4, :]
        squared = stats[p, :, :, 1, 4:8, :] + gap * gap * stats[p, :, :, 0, 4:8, :]
        return alpha, jnp.sqrt(add(squared) / count + EPSILON)

    for t in range(BLK):
        combine(t)

    @pl.when(seg == 0)
    def _():
        end_copy(0).wait()

    @pl.when(seg == segs - 1)
    def _():
        end_copy(1).wait()

    image[...] = jnp.zeros_like(image)

    def apply_first(step, _):
        b = step // CHUNKS
        c = step % CHUNKS

        @pl.when(seg > 0)
        def _():
            env_copy(0, b, c).wait_recv()

        @pl.when(seg < segs - 1)
        def _():
            env_copy(1, b, c).wait_recv()

        image[b] = image[b] + contract(b, c * CHUNK, CHUNK)
        return 0

    lax.fori_loop(0, BLK * CHUNKS, apply_first, 0)
    for t in range(BLK):
        finish(1, t, image[t], sigma0, None)
    for g in range(len(GROUPS)):
        gather_first(1, g)
    stats_first(1)
    stats_second(1)
    for g in range(len(GROUPS)):
        gather_second(1, g)

    lane = lax.broadcasted_iota(jnp.int32, (1, BD), 1)

    def application(k, carry):
        coefs, sigma = carry
        last = k % 2
        p = (k + 1) % 2
        stats_end(last)
        alpha, beta = scalars(last)
        coefs = jnp.where(lane == 2 * k - 2, alpha, coefs)
        coefs = jnp.where(lane == 2 * k - 1, beta, coefs)
        inverse = 1.0 / beta
        local_stats[...] = stats[last, :, :, 1]
        gather_end(last)
        local0[...] = half0[last]
        local1[...] = half1[last]

        for t in range(BLK):
            gap = (alpha - stats[last, 0, 0, 1, t:t + 1, :]) * sigma
            v = own[t].astype(F32)
            before[t] = v * sigma
            for h, ref in ((0, half0), (1, half1)):
                rows = slice(h * HALF, (h + 1) * HALF)
                y = ref[last, t, 0, 0].astype(F32)
                own[t, rows, :] = ((y - gap * v[rows]) * inverse).astype(BF)

        def correct(q, _):
            sub, y, z = place[0, q], place[1, q], place[2, q]
            gap = (alpha - local_stats[y, z, pl.ds(sub, 1), :]) * sigma
            top = local0[sub, y, z].astype(F32) - gap * picked[q, :HALF, :].astype(F32)
            picked[q, :HALF, :] = (top * inverse).astype(BF)
            low = local1[sub, z, y].astype(F32) - gap * picked[q, HALF:, :].astype(F32)
            picked[q, HALF:, :] = (low * inverse).astype(BF)
            return 0

        lax.fori_loop(0, BLK * ENT, correct, 0)

        one = jnp.ones((1, BD), F32)
        for t in range(BLK):
            combine(t)
            finish(p, t, contract(t, 0, CH), one, beta)

        @pl.when(k < APPS - 1)
        def _():
            for g in range(len(GROUPS)):
                gather_first(p, g)

        stats_first(p)
        stats_second(p)

        @pl.when(k < APPS - 1)
        def _():
            for g in range(len(GROUPS)):
                gather_second(p, g)

        return coefs, one

    coefs, _ = lax.fori_loop(1, APPS, application, (jnp.zeros((1, BD), F32), sigma0))

    p = APPS % 2
    stats_end(p)
    alpha, _ = scalars(p)
    coefs = jnp.where(lane == 2 * APPS - 2, alpha, coefs)
    out_coef[...] = coefs[:, :2 * APPS - 1]
    for t in range(BLK):
        out_vector[t] = own[t]
        gap = alpha - stats[p, 0, 0, 1, t:t + 1, :]
        out_rest[t] = leftover[t] - gap * own[t].astype(F32)

    def sent(step, _):
        b = step // CHUNKS
        c = step % CHUNKS

        @pl.when(seg < segs - 1)
        def _():
            env_copy(0, b, c).wait_send()

        @pl.when(seg > 0)
        def _():
            env_copy(1, b, c).wait_send()

        return 0

    lax.fori_loop(0, BLK * CHUNKS, sent, 0)


def on_device(segs, count, psi, env_left, env_right, site_left, site_right, mix_left, mix_right, sources, terms, term_coef, energy):
    vmem = pl.BlockSpec(memory_space=pltpu.VMEM)
    smem = pl.BlockSpec(memory_space=pltpu.SMEM)
    hbm = pl.BlockSpec(memory_space=pl.ANY)
    dma = pltpu.SemaphoreType.DMA
    groups = len(GROUPS)
    vector, rest, coefs = pl.pallas_call(
        functools.partial(kernel, segs, count),
        out_shape=(
            jax.ShapeDtypeStruct((BLK, BD, BD), BF),
            jax.ShapeDtypeStruct((BLK, BD, BD), F32),
            jax.ShapeDtypeStruct((1, 2 * APPS - 1), F32),
        ),
        in_specs=[vmem, hbm, hbm, vmem, vmem, vmem, vmem, smem, smem, vmem, vmem],
        out_specs=(vmem, vmem, vmem),
        scratch_shapes=[
            pltpu.VMEM((2, BLK, CH, BD, BD), BF),
            pltpu.VMEM((2, BLK, CH, BD, BD), BF),
            pltpu.VMEM((2, BLK, CH, BD, BD), BF),
            pltpu.VMEM((CHUNK, BD, BD), BF),
            pltpu.VMEM((2, 2, CH * TILE, CH * TILE), BF),
            pltpu.VMEM((2, BLK, BD, BD), BF),
            pltpu.VMEM((BLK, CH * TILE, 2 * ENT * TILE), BF),
            pltpu.VMEM((BLK, CH, BD, BD), BF),
            pltpu.VMEM((BLK, BD, BD), F32),
            pltpu.VMEM((BLK, BD, BD), F32),
            pltpu.VMEM((BLK * ENT, BD, BD), BF),
            pltpu.VMEM((BLK, BD, BD), BF),
            pltpu.VMEM((BLK, BD, BD), F32),
            pltpu.VMEM((BLK, BD, BD), F32),
            pltpu.VMEM((2, BLK, 4, 4, HALF, BD), BF),
            pltpu.VMEM((2, BLK, 4, 4, HALF, BD), BF),
            pltpu.VMEM((2, 4, 4, 2, 8, BD), F32),
            pltpu.VMEM((BLK, 4, 4, HALF, BD), BF),
            pltpu.VMEM((BLK, 4, 4, HALF, BD), BF),
            pltpu.VMEM((4, 4, 8, BD), F32),
            pltpu.SMEM((3, BLK * ENT), jnp.int32),
            dma((2, BLK + 1)),
            dma((2, BLK, CHUNKS)),
            dma((2, BLK, CHUNKS)),
            dma((2, groups, 2)),
            dma((2, groups, 2)),
            dma((2, groups, 2)),
            dma((2, groups, 2)),
            dma((2, 2)),
            dma((2, 2)),
        ],
        compiler_params=pltpu.CompilerParams(
            collective_id=0, has_side_effects=True, vmem_limit_bytes=56 * 2**20
        ),
        name="lanczos",
    )(
        psi[0], env_left[0], env_right[0], site_left[0], site_right[0], mix_left[0], mix_right[0],
        sources[0], terms[0], term_coef, energy[0],
    )
    return vector[None], rest[None], coefs


def solution(mesh):
    in_specs = (
        P("seg", "sec", None, None),
        P("seg", "sec", None, None, None),
        P("seg", "sec", None, None, None),
        P("seg", "sec", None, None),
        P("seg", "sec", None, None),
        P("seg", None, None),
        P("seg", None, None),
        P("seg", "sec", None),
        P("seg", "sec", None),
        P(),
        P("seg", "sec", None),
    )
    out_specs = (P("seg", "sec", None, None), P("seg", "sec", None, None), P("seg", None))
    segs = mesh.shape["seg"]
    count = float(BLK * mesh.shape["sec"] * BD * BD)
    return jax.shard_map(
        functools.partial(on_device, segs, count), mesh=mesh, in_specs=in_specs, out_specs=out_specs, check_vma=False
    )
```

```python
import functools

import jax
import jax.numpy as jnp
from jax import lax
from jax.experimental import pallas as pl
from jax.experimental.pallas import tpu as pltpu
from jax.sharding import PartitionSpec as P

APPS = 6
EPSILON = 1e-06
CH = 40
BD = 128
ENT = 6
BLK = 3
HALF = BD // 2
TILE = 16
MESH = pl.DeviceIdType.MESH
BF = jnp.bfloat16
F32 = jnp.float32

CHUNK = 8
CHUNKS = CH // CHUNK
LANES = BD // 2
PEERS = tuple((z, y) for z in range(4) for y in range(4) if (z, y) != (0, 0))


def dot(a, b):
    return lax.dot_general(a, b, (((1,), (0,)), ((), ())), preferred_element_type=F32)


def dot_nt(a, b):
    return lax.dot_general(a, b, (((1,), (1,)), ((), ())), preferred_element_type=F32)


def total(x):
    lanes = jnp.sum(x, axis=0, keepdims=True)
    return jnp.broadcast_to(jnp.sum(lanes, axis=1, keepdims=True), (1, BD))


def split(x):
    high = x.astype(BF)
    return high, (x - high.astype(F32)).astype(BF)


def wait_bytes(ref, sem):
    pltpu.make_async_copy(ref, ref, sem).wait()


def spread(rows, start):
    row = lax.broadcasted_iota(jnp.int32, (rows, CH), 0) + start
    return (row // TILE == lax.broadcasted_iota(jnp.int32, (rows, CH), 1)).astype(BF)


def same_state(rows, cols):
    row = lax.broadcasted_iota(jnp.int32, (rows, cols), 0)
    col = lax.broadcasted_iota(jnp.int32, (rows, cols), 1)
    return row % TILE == col % TILE


def kernel(
    segs,
    count,
    psi,
    env_left,
    env_right,
    site_left,
    site_right,
    mix_left,
    mix_right,
    sources,
    terms,
    term_coef,
    energy,
    out_vector,
    out_rest,
    out_coef,
    env_in,
    grown,
    envs,
    mixed,
    mix_kron,
    pattern,
    chooser,
    site_t,
    term_kron,
    combo,
    image,
    on_site,
    picked,
    own,
    before,
    leftover,
    half0,
    half1,
    stats,
    local0,
    local1,
    local_stats,
    place,
    load_sem,
    env_send,
    env_recv,
    s1,
    r1,
    s2,
    r2,
    stat_send,
    stat_recv,
):
    seg = lax.axis_index("seg")
    sec = lax.axis_index("sec")
    my_z = sec // 4
    my_y = sec % 4

    def along_z(d):
        return (seg, ((my_z + d) % 4) * 4 + my_y)

    def along_y(d):
        return (seg, my_z * 4 + (my_y + d) % 4)

    def along_both(dz, dy):
        return (seg, ((my_z + dz) % 4) * 4 + (my_y + dy) % 4)

    def send(src, dst, ssem, rsem, device):
        pltpu.make_async_remote_copy(
            src_ref=src, dst_ref=dst, send_sem=ssem, recv_sem=rsem,
            device_id=device, device_id_type=MESH,
        ).start()

    loads = []
    for b in range(BLK):
        for side, ref in ((0, env_left), (1, env_right)):
            c = pltpu.make_async_copy(ref.at[b], env_in.at[side, b], load_sem.at[side, b])
            c.start()
            loads.append(c)

    for p in range(2):
        stats[p, 0] = jnp.zeros((8, BD), F32)

    barrier = pltpu.get_barrier_semaphore()
    for dz, dy in PEERS:
        pl.semaphore_signal(barrier, inc=1, device_id=along_both(dz, dy), device_id_type=MESH)

    @pl.when(seg > 0)
    def _():
        pl.semaphore_signal(barrier, inc=1, device_id=(seg - 1, sec), device_id_type=MESH)

    @pl.when(seg < segs - 1)
    def _():
        pl.semaphore_signal(barrier, inc=1, device_id=(seg + 1, sec), device_id_type=MESH)

    def end_copy(side):
        source = env_left if side == 0 else env_right
        return pltpu.make_async_copy(source, envs.at[side], load_sem.at[side, BLK])

    @pl.when(seg == 0)
    def _():
        end_copy(0).start()

    @pl.when(seg == segs - 1)
    def _():
        end_copy(1).start()

    pattern[...] = jnp.where(same_state(BD, CH * TILE), 1.0, 0.0).astype(BF)
    chooser[...] = spread(CH * TILE, 0)

    def spread_mix(side, c, rows):
        ref = mix_left if side == 0 else mix_right
        chosen = chooser[rows, :]
        for part, mix in enumerate(split(ref[...])):
            full = dot_nt(dot(chosen, mix).astype(BF), chooser[...])
            mix_kron[side, part, rows, :] = full.astype(BF) * pattern[...]

    eye_row = lax.broadcasted_iota(jnp.int32, (BD, BD), 0)
    eye = (eye_row == lax.broadcasted_iota(jnp.int32, (BD, BD), 1)).astype(BF)
    for side, ref in ((0, site_left), (1, site_right)):
        for b in range(BLK):
            site_t[side, b] = dot_nt(eye, ref[b]).astype(BF)

    for t in range(BLK):
        half0[0, t, 0, 0] = psi[t, :HALF, :]
        half1[0, t, 0, 0] = psi[t, HALF:, :]
        own[t] = psi[t]

    pl.semaphore_wait(
        barrier, len(PEERS) + jnp.where(seg > 0, 1, 0) + jnp.where(seg < segs - 1, 1, 0)
    )

    def gather_first(p, t):
        for d in (1, 3, 2):
            back = (4 - d) % 4
            send(half0.at[p, t, 0, 0], half0.at[p, t, 0, back], s1.at[p, t, 0], r1.at[p, t, 0], along_z(d))
            send(half1.at[p, t, 0, 0], half1.at[p, t, 0, back], s1.at[p, t, 1], r1.at[p, t, 1], along_y(d))

    def gather_second(p, t):
        for h, ref, along in ((0, half0, along_y), (1, half1, along_z)):
            wait_bytes(ref.at[p, t, 0, pl.ds(1, 3)], r1.at[p, t, h])
            for d in (1, 3, 2):
                back = (4 - d) % 4
                send(ref.at[p, t, 0], ref.at[p, t, back], s2.at[p, t, h], r2.at[p, t, h], along(d))

    def gather_end(p, t):
        for h, ref, local in ((0, half0, local0), (1, half1, local1)):
            wait_bytes(ref.at[p, t, pl.ds(1, 3)], r2.at[p, t, h])
            local[t] = ref[p, t]
            wait_bytes(ref.at[p, t, 0, pl.ds(1, 3)], s1.at[p, t, h])
            wait_bytes(ref.at[p, t, pl.ds(1, 3)], s2.at[p, t, h])

    def stats_first(p):
        for dz, dy in PEERS:
            back = (4 - dy) % 4 * 4 + (4 - dz) % 4
            send(stats.at[p, 0], stats.at[p, back], stat_send.at[p], stat_recv.at[p], along_both(dz, dy))

    def stats_end(p):
        wait_bytes(stats.at[p, pl.ds(1, 15)], stat_recv.at[p])
        wait_bytes(stats.at[p, pl.ds(1, 15)], stat_send.at[p])

    for t in range(BLK):
        gather_first(0, t)

    def env_copy(side, b, c):
        part = pl.ds(c * CHUNK, CHUNK)
        to = seg + 1 if side == 0 else seg - 1
        return pltpu.make_async_remote_copy(
            src_ref=grown.at[side, b, part],
            dst_ref=envs.at[side, b, part],
            send_sem=env_send.at[side, b, c],
            recv_sem=env_recv.at[side, b, c],
            device_id=(to, sec),
            device_id_type=MESH,
        )

    def grow(step, _):
        b = step // CHUNKS
        c = step % CHUNKS
        for side, site in ((0, site_left), (1, site_right)):
            @pl.when(c == 0)
            def _(side=side):
                wait_bytes(env_in.at[side, b], load_sem.at[side, b])

            rows = pl.ds(pl.multiple_of(c * CHUNK * TILE, CHUNK * TILE), CHUNK * TILE)

            @pl.when(b == 0)
            def _(side=side, rows=rows):
                spread_mix(side, c, rows)

            high = mix_kron[side, 0, rows, :]
            low = mix_kron[side, 1, rows, :]
            for i in range(BD // (2 * TILE)):
                base = i * 2 * TILE
                cols = [
                    env_in[side, b, :, base + h * TILE:base + (h + 1) * TILE, :].reshape(CH * TILE, BD)
                    for h in range(2)
                ]
                both = jnp.concatenate(cols, axis=1)
                out = (dot(high, both) + dot(low, both)).astype(BF)
                for h in range(2):
                    mixed[:, base + h * TILE:base + (h + 1) * TILE, :] = out[:, h * BD:(h + 1) * BD].reshape(
                        CHUNK, TILE, BD
                    )
            half = dot(mixed[...].reshape(CHUNK * BD, BD), site[b]).astype(BF)
            wide = jnp.concatenate([half[v * BD:(v + 1) * BD] for v in range(CHUNK)], axis=1)
            done = dot(site_t[side, b], wide).astype(BF)
            for v in range(CHUNK):
                grown[side, b, c * CHUNK + v] = done[:, v * BD:(v + 1) * BD]

            @pl.when(seg < segs - 1 if side == 0 else seg > 0)
            def _(side=side):
                env_copy(side, b, c).start()

        return 0

    lax.fori_loop(0, BLK * CHUNKS, grow, 0)

    for t in range(BLK):
        gather_second(0, t)

    for t in range(BLK):
        row = jnp.broadcast_to(energy[t], (BD, BD))
        on_site[t] = jnp.transpose(row)
    spread_all = spread(CH * TILE, 0)
    keep = same_state(CH * TILE, ENT * TILE)
    for t in range(BLK):
        entry = lax.broadcasted_iota(jnp.int32, (8, ENT * TILE), 1) // TILE
        kind = jnp.zeros((8, ENT * TILE), jnp.int32)
        for k in range(ENT):
            kind = jnp.where(entry == k, terms[t, 0, k], kind)
        hit = (kind == lax.broadcasted_iota(jnp.int32, (8, ENT * TILE), 0)).astype(BF)
        for part, coef in enumerate(split(term_coef[...])):
            rows = dot_nt(spread_all, coef).astype(BF)
            full = dot(rows, hit)
            term_kron[t, :, part * ENT * TILE:(part + 1) * ENT * TILE] = jnp.where(keep, full, 0.0).astype(BF)

    def where_is(t, k):
        s = sources[t, 0, k]
        owner = s // BLK
        sub = s - BLK * owner
        return sub, (owner % 4 - my_y + 4) % 4, (owner // 4 - my_z + 4) % 4

    for t in range(BLK):
        for k in range(ENT):
            for n, value in enumerate(where_is(t, k)):
                place[n, t * ENT + k] = value

    for t in range(BLK):
        gather_end(0, t)

    def fetch(q, _):
        sub, y, z = place[0, q], place[1, q], place[2, q]
        picked[q, :HALF, :] = local0[sub, y, z]
        picked[q, HALF:, :] = local1[sub, z, y]
        return 0

    lax.fori_loop(0, BLK * ENT, fetch, 0)

    def squares(n, acc):
        t, o = n // 4, n % 4
        for i in range(4):
            for ref in (local0, local1):
                x = ref[t, o, i].astype(F32)
                acc = acc + x * x
        return acc

    norm = total(lax.fori_loop(0, BLK * 4, squares, jnp.zeros((HALF, BD), F32)))
    sigma0 = 1.0 / jnp.sqrt(norm / count + EPSILON)

    lane = lax.broadcasted_iota(jnp.int32, (1, BD), 1)

    def combine(t):
        for i in range(BD // (2 * TILE)):
            base = i * 2 * TILE
            cols = [
                picked[t * ENT:(t + 1) * ENT, base + h * TILE:base + (h + 1) * TILE, :].reshape(ENT * TILE, BD)
                for h in range(2)
            ]
            both = jnp.concatenate(cols, axis=1)
            out = dot(term_kron[t], jnp.concatenate([both, both], axis=0)).astype(BF)
            for h in range(2):
                combo[t, :, base + h * TILE:base + (h + 1) * TILE, :] = out[:, h * BD:(h + 1) * BD].reshape(
                    CH, TILE, BD
                )

    def contract(t, first, n):
        inner = [dot(envs[0, t, first + j], combo[t, first + j]).astype(BF) for j in range(n)]
        right = [envs[1, t, first + j] for j in range(n)]
        return dot_nt(jnp.concatenate(inner, axis=1), jnp.concatenate(right, axis=1))

    def finish(p, t, applied, sigma, beta):
        v = own[t].astype(F32) * sigma
        img = applied * sigma + on_site[t] * v
        w = img if beta is None else img - beta * before[t]
        prod = total(img * v)
        norm = total(v * v)
        over = total(w * v)
        a = jnp.where(norm > 0.0, over / jnp.where(norm > 0.0, norm, 1.0), 0.0)
        y = w - a * v
        leftover[t] = y
        low = y.astype(BF)
        half0[p, t, 0, 0] = low[:HALF]
        half1[p, t, 0, 0] = low[HALF:]
        stats[p, 0, t:t + 1, :] = jnp.where(lane < LANES, prod, norm)
        stats[p, 0, 4 + t:5 + t, :] = jnp.where(lane < LANES, a, total(y * y))

    def scalars(p):
        def add(x):
            lines = jnp.sum(x.reshape(16, 4, BD), axis=0)
            return jnp.sum(lines, axis=0, keepdims=True)

        got = stats[p]
        turned = pltpu.roll(got.reshape(16 * 8, BD), LANES, 1).reshape(16, 8, BD)
        first = jnp.where(lane < LANES, got, turned)
        second = jnp.where(lane < LANES, turned, got)
        local_stats[...] = first
        alpha = add(first[:, 0:4, :]) / count
        gap = alpha - first[:, 4:8, :]
        squared = second[:, 4:8, :] + gap * gap * second[:, 0:4, :]
        return alpha, jnp.sqrt(add(squared) / count + EPSILON)

    for t in range(BLK):
        combine(t)

    @pl.when(seg == 0)
    def _():
        end_copy(0).wait()

    @pl.when(seg == segs - 1)
    def _():
        end_copy(1).wait()

    image[...] = jnp.zeros_like(image)

    for b in range(BLK):
        def apply_first(c, _, b=b):
            @pl.when(seg > 0)
            def _():
                env_copy(0, b, c).wait_recv()

            @pl.when(seg < segs - 1)
            def _():
                env_copy(1, b, c).wait_recv()

            image[b] = image[b] + contract(b, c * CHUNK, CHUNK)
            return 0

        lax.fori_loop(0, CHUNKS, apply_first, 0)
        finish(1, b, image[b], sigma0, None)
        if b == BLK - 1:
            stats_first(1)
        gather_first(1, b)
        if b > 0:
            gather_second(1, b - 1)
    gather_second(1, BLK - 1)

    def application(k, carry):
        coefs, sigma = carry
        last = k % 2
        p = (k + 1) % 2
        stats_end(last)
        alpha, beta = scalars(last)
        coefs = jnp.where(lane == 2 * k - 2, alpha, coefs)
        coefs = jnp.where(lane == 2 * k - 1, beta, coefs)
        inverse = 1.0 / beta
        for t in range(BLK):
            gather_end(last, t)

        for t in range(BLK):
            gap = (alpha - local_stats[0, 4 + t:5 + t, :]) * sigma
            v = own[t].astype(F32)
            before[t] = v * sigma
            for h, ref in ((0, local0), (1, local1)):
                rows = slice(h * HALF, (h + 1) * HALF)
                y = ref[t, 0, 0].astype(F32)
                own[t, rows, :] = ((y - gap * v[rows]) * inverse).astype(BF)

        def correct(q, _):
            sub, y, z = place[0, q], place[1, q], place[2, q]
            gap = (alpha - local_stats[y * 4 + z, pl.ds(4 + sub, 1), :]) * sigma
            top = local0[sub, y, z].astype(F32) - gap * picked[q, :HALF, :].astype(F32)
            picked[q, :HALF, :] = (top * inverse).astype(BF)
            low = local1[sub, z, y].astype(F32) - gap * picked[q, HALF:, :].astype(F32)
            picked[q, HALF:, :] = (low * inverse).astype(BF)
            return 0

        lax.fori_loop(0, BLK * ENT, correct, 0)

        one = jnp.ones((1, BD), F32)
        for t in range(BLK):
            combine(t)
            finish(p, t, contract(t, 0, CH), one, beta)
            if t == BLK - 1:
                stats_first(p)

            @pl.when(k < APPS - 1)
            def _(t=t):
                gather_first(p, t)
                if t > 0:
                    gather_second(p, t - 1)
                if t == BLK - 1:
                    gather_second(p, t)

        return coefs, one

    coefs, _ = lax.fori_loop(1, APPS, application, (jnp.zeros((1, BD), F32), sigma0))

    p = APPS % 2
    stats_end(p)
    alpha, _ = scalars(p)
    coefs = jnp.where(lane == 2 * APPS - 2, alpha, coefs)
    out_coef[...] = coefs[:, :2 * APPS - 1]
    for t in range(BLK):
        out_vector[t] = own[t]
        gap = alpha - local_stats[0, 4 + t:5 + t, :]
        out_rest[t] = leftover[t] - gap * own[t].astype(F32)

    def sent(step, _):
        b = step // CHUNKS
        c = step % CHUNKS

        @pl.when(seg < segs - 1)
        def _():
            env_copy(0, b, c).wait_send()

        @pl.when(seg > 0)
        def _():
            env_copy(1, b, c).wait_send()

        return 0

    lax.fori_loop(0, BLK * CHUNKS, sent, 0)


def move(*refs):
    for i in range(3):
        refs[3 + i][...] = refs[i][...]


def hand_on(*arrays):
    hbm = pl.BlockSpec(memory_space=pltpu.VMEM)
    return pl.pallas_call(
        move,
        out_shape=tuple(jax.ShapeDtypeStruct(a.shape, a.dtype) for a in arrays),
        in_specs=[hbm] * 3,
        out_specs=(hbm,) * 3,
        name="hand_on",
    )(*arrays)


def on_device(segs, count, psi, env_left, env_right, site_left, site_right, mix_left, mix_right, sources, terms, term_coef, energy):
    vmem = pl.BlockSpec(memory_space=pltpu.VMEM)
    smem = pl.BlockSpec(memory_space=pltpu.SMEM)
    hbm = pl.BlockSpec(memory_space=pl.ANY)
    dma = pltpu.SemaphoreType.DMA
    vector, rest, coefs = pl.pallas_call(
        functools.partial(kernel, segs, count),
        out_shape=(
            jax.ShapeDtypeStruct((BLK, BD, BD), BF),
            jax.ShapeDtypeStruct((BLK, BD, BD), F32),
            jax.ShapeDtypeStruct((1, 2 * APPS - 1), F32),
        ),
        in_specs=[vmem, hbm, hbm, vmem, vmem, vmem, vmem, smem, smem, vmem, vmem],
        out_specs=(vmem, vmem, vmem),
        scratch_shapes=[
            pltpu.VMEM((2, BLK, CH, BD, BD), BF),
            pltpu.VMEM((2, BLK, CH, BD, BD), BF),
            pltpu.VMEM((2, BLK, CH, BD, BD), BF),
            pltpu.VMEM((CHUNK, BD, BD), BF),
            pltpu.VMEM((2, 2, CH * TILE, CH * TILE), BF),
            pltpu.VMEM((BD, CH * TILE), BF),
            pltpu.VMEM((CH * TILE, CH), BF),
            pltpu.VMEM((2, BLK, BD, BD), BF),
            pltpu.VMEM((BLK, CH * TILE, 2 * ENT * TILE), BF),
            pltpu.VMEM((BLK, CH, BD, BD), BF),
            pltpu.VMEM((BLK, BD, BD), F32),
            pltpu.VMEM((BLK, BD, BD), F32),
            pltpu.VMEM((BLK * ENT, BD, BD), BF),
            pltpu.VMEM((BLK, BD, BD), BF),
            pltpu.VMEM((BLK, BD, BD), F32),
            pltpu.VMEM((BLK, BD, BD), F32),
            pltpu.VMEM((2, BLK, 4, 4, HALF, BD), BF),
            pltpu.VMEM((2, BLK, 4, 4, HALF, BD), BF),
            pltpu.VMEM((2, 16, 8, BD), F32),
            pltpu.VMEM((BLK, 4, 4, HALF, BD), BF),
            pltpu.VMEM((BLK, 4, 4, HALF, BD), BF),
            pltpu.VMEM((16, 8, BD), F32),
            pltpu.SMEM((3, BLK * ENT), jnp.int32),
            dma((2, BLK + 1)),
            dma((2, BLK, CHUNKS)),
            dma((2, BLK, CHUNKS)),
            dma((2, BLK, 2)),
            dma((2, BLK, 2)),
            dma((2, BLK, 2)),
            dma((2, BLK, 2)),
            dma((2,)),
            dma((2,)),
        ],
        compiler_params=pltpu.CompilerParams(
            collective_id=0, has_side_effects=True, vmem_limit_bytes=56 * 2**20
        ),
        name="lanczos",
    )(
        psi[0], env_left[0], env_right[0], site_left[0], site_right[0], mix_left[0], mix_right[0],
        jnp.transpose(sources, (1, 0, 2)), jnp.transpose(terms, (1, 0, 2)), term_coef, jnp.transpose(energy, (1, 0, 2)),
    )
    vector, rest, coefs = hand_on(vector, rest, coefs)
    return vector[None], rest[None], coefs


def solution(mesh):
    in_specs = (
        P("seg", "sec", None, None),
        P("seg", "sec", None, None, None),
        P("seg", "sec", None, None, None),
        P("seg", "sec", None, None),
        P("seg", "sec", None, None),
        P("seg", None, None),
        P("seg", None, None),
        P("seg", "sec", None),
        P("seg", "sec", None),
        P(),
        P("seg", "sec", None),
    )
    out_specs = (P("seg", "sec", None, None), P("seg", "sec", None, None), P("seg", None))
    segs = mesh.shape["seg"]
    count = float(BLK * mesh.shape["sec"] * BD * BD)
    return jax.shard_map(
        functools.partial(on_device, segs, count), mesh=mesh, in_specs=in_specs, out_specs=out_specs, check_vma=False
    )
```

```python
import functools

import jax
import jax.numpy as jnp
from jax import lax
from jax.experimental import pallas as pl
from jax.experimental.pallas import tpu as pltpu
from jax.sharding import PartitionSpec as P

APPS = 6
EPSILON = 1e-06
CH = 40
BD = 128
ENT = 6
BLK = 3
HALF = BD // 2
TILE = 16
BY_ID = pl.DeviceIdType.LOGICAL
BF = jnp.bfloat16
F32 = jnp.float32

CHUNK = 8
CHUNKS = CH // CHUNK
LANES = BD // 2
ROWS = BD + TILE
PEERS = tuple((z, y) for z in range(4) for y in range(4) if (z, y) != (0, 0))


def dot(a, b):
    return lax.dot_general(a, b, (((1,), (0,)), ((), ())), preferred_element_type=F32)


def dot_nt(a, b):
    return lax.dot_general(a, b, (((1,), (1,)), ((), ())), preferred_element_type=F32)


def total(x):
    lanes = jnp.sum(x, axis=0, keepdims=True)
    return jnp.broadcast_to(jnp.sum(lanes, axis=1, keepdims=True), (1, BD))


def split(x):
    high = x.astype(BF)
    return high, (x - high.astype(F32)).astype(BF)


def wait_bytes(ref, sem):
    pltpu.make_async_copy(ref, ref, sem).wait()


def spread(rows, start):
    row = lax.broadcasted_iota(jnp.int32, (rows, CH), 0) + start
    return (row // TILE == lax.broadcasted_iota(jnp.int32, (rows, CH), 1)).astype(BF)


def same_state(rows, cols):
    row = lax.broadcasted_iota(jnp.int32, (rows, cols), 0)
    col = lax.broadcasted_iota(jnp.int32, (rows, cols), 1)
    return row % TILE == col % TILE


def kernel(
    segs,
    count,
    psi,
    env_left,
    env_right,
    site_left,
    site_right,
    mix_left,
    mix_right,
    sources,
    terms,
    term_coef,
    energy,
    out_vector,
    out_rest,
    out_coef,
    env_in,
    grown,
    envs,
    mixed,
    mix_kron,
    mix_parts,
    sites,
    pattern,
    chooser,
    site_t,
    term_kron,
    combo,
    image,
    on_site,
    picked,
    own,
    before,
    leftover,
    pieces,
    stats,
    local,
    facts,
    place,
    load_sem,
    env_send,
    env_recv,
    ssem,
    rsem,
    stat_send,
    stat_recv,
):
    seg = lax.axis_index("seg")
    sec = lax.axis_index("sec")
    my_z = sec // 4
    my_y = sec % 4

    def at(z, y):
        return seg * 16 + z * 4 + y

    to_z = {d: at((my_z + d) % 4, my_y) for d in (1, 2, 3)}
    to_y = {d: at(my_z, (my_y + d) % 4) for d in (1, 2, 3)}
    to_peer = {(dz, dy): at((my_z + dz) % 4, (my_y + dy) % 4) for dz, dy in PEERS}
    here = at(my_z, my_y)

    def send(src, dst, ssem, rsem, device):
        pltpu.make_async_remote_copy(
            src_ref=src, dst_ref=dst, send_sem=ssem, recv_sem=rsem,
            device_id=device, device_id_type=BY_ID,
        ).start()

    loads = []
    for b in range(BLK):
        for side, ref in ((0, env_left), (1, env_right)):
            c = pltpu.make_async_copy(ref.at[b], env_in.at[side, b], load_sem.at[side, b])
            c.start()
            loads.append(c)

    stats[0] = jnp.zeros((8, BD), F32)

    barrier = pltpu.get_barrier_semaphore()
    for dz, dy in PEERS:
        pl.semaphore_signal(barrier, inc=1, device_id=to_peer[dz, dy], device_id_type=BY_ID)

    @pl.when(seg > 0)
    def _():
        pl.semaphore_signal(barrier, inc=1, device_id=here - 16, device_id_type=BY_ID)

    @pl.when(seg < segs - 1)
    def _():
        pl.semaphore_signal(barrier, inc=1, device_id=here + 16, device_id_type=BY_ID)

    def end_copy(side):
        source = env_left if side == 0 else env_right
        return pltpu.make_async_copy(source, envs.at[side], load_sem.at[side, BLK])

    @pl.when(seg == 0)
    def _():
        end_copy(0).start()

    @pl.when(seg == segs - 1)
    def _():
        end_copy(1).start()

    pattern[...] = jnp.where(same_state(BD, CH * TILE), 1.0, 0.0).astype(BF)
    chooser[...] = spread(CH * TILE, 0)

    for side, (mix, site) in enumerate(((mix_left, site_left), (mix_right, site_right))):
        for part, value in enumerate(split(mix[...])):
            mix_parts[side, part] = value
        sites[side] = site[...]

    def spread_mix(side, rows):
        chosen = chooser[rows, :]
        for part in range(2):
            full = dot_nt(dot(chosen, mix_parts[side, part]).astype(BF), chooser[...])
            at = slice(part * CH * TILE, (part + 1) * CH * TILE)
            mix_kron[side, rows, at] = full.astype(BF) * pattern[...]

    eye_row = lax.broadcasted_iota(jnp.int32, (BD, BD), 0)
    eye = (eye_row == lax.broadcasted_iota(jnp.int32, (BD, BD), 1)).astype(BF)
    for side, ref in ((0, site_left), (1, site_right)):
        for b in range(BLK):
            site_t[side, b] = dot_nt(eye, ref[b]).astype(BF)

    for t in range(BLK):
        pieces[0, t, 0, 0, :BD, :] = psi[t]
        pieces[0, t, 0, 0, BD:, :] = jnp.zeros((TILE, BD), BF)
        own[t] = psi[t]

    pl.semaphore_wait(
        barrier, len(PEERS) + jnp.where(seg > 0, 1, 0) + jnp.where(seg < segs - 1, 1, 0)
    )

    axes = ((0, to_y, pl.ds(0, HALF)), (1, to_z, pl.ds(HALF, ROWS - HALF)))

    def direct(p, t, h):
        return pieces.at[p, t, 0, pl.ds(1, 3)] if h == 0 else pieces.at[p, t, pl.ds(1, 3), 0]

    def bundle(p, t, h, o, rows):
        return pieces.at[p, t, o, pl.ds(1, 3), rows] if h == 0 else pieces.at[p, t, pl.ds(1, 3), o, rows]

    def gather_first(p, t):
        mine = pieces.at[p, t, 0, 0]
        for d in (1, 3, 2):
            back = (4 - d) % 4
            send(mine, pieces.at[p, t, 0, back], ssem.at[p, t, 0, 0], rsem.at[p, t, 0, 0], to_z[d])
            send(mine, pieces.at[p, t, back, 0], ssem.at[p, t, 1, 0], rsem.at[p, t, 1, 0], to_y[d])

    def gather_second(p, t):
        for h, to, rows in axes:
            wait_bytes(direct(p, t, h), rsem.at[p, t, h, 0])
            for d in (1, 3, 2):
                back = (4 - d) % 4
                send(bundle(p, t, h, 0, rows), bundle(p, t, h, back, rows), ssem.at[p, t, h, 1], rsem.at[p, t, h, 1], to[d])

    def gather_end(p, t):
        for h, _, rows in axes:
            wait_bytes(pieces.at[p, t, pl.ds(1, 3), pl.ds(1, 3), rows], rsem.at[p, t, h, 1])
        local[t] = pieces[p, t]

    def gather_sent(p, t):
        for h, _, rows in axes:
            wait_bytes(direct(p, t, h), ssem.at[p, t, h, 0])
            wait_bytes(pieces.at[p, t, pl.ds(1, 3), pl.ds(1, 3), rows], ssem.at[p, t, h, 1])

    def gather_onward(p, t):
        if t > 0:
            gather_second(p, t - 1)
        if t == BLK - 1:
            gather_second(p, t)

    def stats_send():
        for dz, dy in PEERS:
            back = (4 - dy) % 4 * 4 + (4 - dz) % 4
            send(stats.at[0], stats.at[back], stat_send, stat_recv, to_peer[dz, dy])

    def stats_end():
        wait_bytes(stats.at[pl.ds(1, 15)], stat_recv)
        wait_bytes(stats.at[pl.ds(1, 15)], stat_send)

    def env_copy(side, b, c):
        part = pl.ds(c * CHUNK, CHUNK)
        to = here + 16 - 32 * side
        return pltpu.make_async_remote_copy(
            src_ref=grown.at[side, b, part],
            dst_ref=envs.at[side, b, part],
            send_sem=env_send.at[side, b, c],
            recv_sem=env_recv.at[side, b, c],
            device_id=to,
            device_id_type=BY_ID,
        )

    def grow(step, _):
        side = (step + 1 + seg) % 2
        b = step // 2 // CHUNKS
        c = step // 2 % CHUNKS
        rows = pl.ds(pl.multiple_of(c * CHUNK * TILE, CHUNK * TILE), CHUNK * TILE)

        @pl.when(c == 0)
        def _():
            wait_bytes(env_in.at[side, b], load_sem.at[side, b])

        @pl.when(b == 0)
        def _():
            spread_mix(side, rows)

        maps = mix_kron[side, rows, :]
        for i in range(BD // (2 * TILE)):
            base = i * 2 * TILE
            cols = [
                env_in[side, b, :, base + h * TILE:base + (h + 1) * TILE, :].reshape(CH * TILE, BD)
                for h in range(2)
            ]
            both = jnp.concatenate(cols, axis=1)
            out = dot(maps, jnp.concatenate([both, both], axis=0)).astype(BF)
            for h in range(2):
                mixed[:, base + h * TILE:base + (h + 1) * TILE, :] = out[:, h * BD:(h + 1) * BD].reshape(
                    CHUNK, TILE, BD
                )
        half = dot(mixed[...].reshape(CHUNK * BD, BD), sites[side, b]).astype(BF)
        wide = jnp.concatenate([half[v * BD:(v + 1) * BD] for v in range(CHUNK)], axis=1)
        done = dot(site_t[side, b], wide).astype(BF)
        for v in range(CHUNK):
            grown[side, b, c * CHUNK + v] = done[:, v * BD:(v + 1) * BD]

        @pl.when(jnp.where(side == 0, seg < segs - 1, seg > 0))
        def _():
            env_copy(side, b, c).start()

        return 0

    lax.fori_loop(0, 2 * CHUNKS, grow, 0)
    for t in range(BLK):
        gather_first(0, t)
    lax.fori_loop(2 * CHUNKS, 4 * CHUNKS, grow, 0)
    for t in range(BLK):
        gather_second(0, t)
    lax.fori_loop(4 * CHUNKS, 6 * CHUNKS, grow, 0)

    for t in range(BLK):
        row = jnp.broadcast_to(energy[t], (BD, BD))
        on_site[t] = jnp.transpose(row)
    spread_all = spread(CH * TILE, 0)
    keep = same_state(CH * TILE, ENT * TILE)
    for t in range(BLK):
        entry = lax.broadcasted_iota(jnp.int32, (8, ENT * TILE), 1) // TILE
        kind = jnp.zeros((8, ENT * TILE), jnp.int32)
        for k in range(ENT):
            kind = jnp.where(entry == k, terms[t, 0, k], kind)
        hit = (kind == lax.broadcasted_iota(jnp.int32, (8, ENT * TILE), 0)).astype(BF)
        for part, coef in enumerate(split(term_coef[...])):
            rows = dot_nt(spread_all, coef).astype(BF)
            full = dot(rows, hit)
            term_kron[t, :, part * ENT * TILE:(part + 1) * ENT * TILE] = jnp.where(keep, full, 0.0).astype(BF)

    def where_is(t, k):
        s = sources[t, 0, k]
        owner = s // BLK
        sub = s - BLK * owner
        return sub, (owner % 4 - my_y + 4) % 4, (owner // 4 - my_z + 4) % 4

    for t in range(BLK):
        for k in range(ENT):
            for n, value in enumerate(where_is(t, k)):
                place[n, t * ENT + k] = value

    for t in range(BLK):
        gather_end(0, t)
        gather_sent(0, t)

    def fetch(q, _):
        sub, y, z = place[0, q], place[1, q], place[2, q]
        picked[q] = local[sub, y, z, :BD, :]
        return 0

    lax.fori_loop(0, BLK * ENT, fetch, 0)

    def squares(n, acc):
        t, o = n // 4, n % 4
        for i in range(4):
            x = local[t, o, i, :BD, :].astype(F32)
            acc = acc + x * x
        return acc

    norm = total(lax.fori_loop(0, BLK * 4, squares, jnp.zeros((BD, BD), F32)))
    sigma0 = 1.0 / jnp.sqrt(norm / count + EPSILON)

    lane = lax.broadcasted_iota(jnp.int32, (1, BD), 1)

    def combine(t):
        for i in range(BD // (2 * TILE)):
            base = i * 2 * TILE
            cols = [
                picked[t * ENT:(t + 1) * ENT, base + h * TILE:base + (h + 1) * TILE, :].reshape(ENT * TILE, BD)
                for h in range(2)
            ]
            both = jnp.concatenate(cols, axis=1)
            out = dot(term_kron[t], jnp.concatenate([both, both], axis=0)).astype(BF)
            for h in range(2):
                combo[t, :, base + h * TILE:base + (h + 1) * TILE, :] = out[:, h * BD:(h + 1) * BD].reshape(
                    CH, TILE, BD
                )

    def contract(t, first, n):
        inner = [dot(envs[0, t, first + j], combo[t, first + j]).astype(BF) for j in range(n)]
        right = [envs[1, t, first + j] for j in range(n)]
        return dot_nt(jnp.concatenate(inner, axis=1), jnp.concatenate(right, axis=1))

    def finish(p, t, applied, sigma, beta, final=False):
        v = own[t].astype(F32) * sigma
        img = applied * sigma + on_site[t] * v
        w = img if beta is None else img - beta * before[t]
        prod = total(img * v)
        norm = total(v * v)
        over = total(w * v)
        a = jnp.where(norm > 0.0, over / jnp.where(norm > 0.0, norm, 1.0), 0.0)
        y = w - a * v
        if final:
            leftover[t] = w
            stats[0, t:t + 1, :] = prod
            return
        pieces[p, t, 0, 0, :BD, :] = y.astype(BF)
        row = lax.broadcasted_iota(jnp.int32, (TILE, BD), 0)
        kind = row % 4
        value = jnp.where(kind == 0, prod, jnp.where(kind == 1, norm, jnp.where(kind == 2, a, total(y * y))))
        one = value.astype(BF).astype(F32)
        two = (value - one).astype(BF).astype(F32)
        three = (value - one - two).astype(BF).astype(F32)
        tile = jnp.where(row < 4, one, jnp.where(row < 8, two, jnp.where(row < 12, three, 0.0)))
        pieces[p, t, 0, 0, BD:, :] = tile.astype(BF)

    def learn(t):
        parts = local[t, :, :, BD:, :].astype(F32).reshape(16, TILE, BD)
        facts[t] = parts[:, 0:4, :] + parts[:, 4:8, :] + parts[:, 8:12, :]

    def scalars():
        alpha = jnp.zeros((1, BD), F32)
        for t in range(BLK):
            alpha = alpha + jnp.sum(facts[t], axis=0)[0:1, :]
        alpha = alpha / count
        squared = jnp.zeros((1, BD), F32)
        for t in range(BLK):
            gap = alpha - facts[t, :, 2, :]
            new = facts[t, :, 3, :] + gap * gap * facts[t, :, 1, :]
            squared = squared + jnp.sum(new, axis=0, keepdims=True)
        return alpha, jnp.sqrt(squared / count + EPSILON)

    for t in range(BLK):
        combine(t)

    @pl.when(seg == 0)
    def _():
        end_copy(0).wait()

    @pl.when(seg == segs - 1)
    def _():
        end_copy(1).wait()

    image[...] = jnp.zeros_like(image)

    for b in range(BLK):
        def apply_first(c, _, b=b):
            @pl.when(seg > 0)
            def _():
                env_copy(0, b, c).wait_recv()

            @pl.when(seg < segs - 1)
            def _():
                env_copy(1, b, c).wait_recv()

            image[b] = image[b] + contract(b, c * CHUNK, CHUNK)
            return 0

        lax.fori_loop(0, CHUNKS, apply_first, 0)
        finish(1, b, image[b], sigma0, None)
        gather_first(1, b)
        gather_onward(1, b)

    def application(k, coefs, sigma, final):
        last = k % 2
        p = (k + 1) % 2
        for t in range(BLK):
            gather_end(last, t)
            learn(t)
        alpha, beta = scalars()
        coefs = jnp.where(lane == 2 * k - 2, alpha, coefs)
        coefs = jnp.where(lane == 2 * k - 1, beta, coefs)
        inverse = 1.0 / beta

        def correct(q, _):
            sub, y, z = place[0, q], place[1, q], place[2, q]
            gap = (alpha - facts[sub, y * 4 + z, 2:3, :]) * sigma
            new = local[sub, y, z, :BD, :].astype(F32) - gap * picked[q].astype(F32)
            picked[q] = (new * inverse).astype(BF)
            return 0

        one = jnp.ones((1, BD), F32)
        for t in range(BLK):
            lax.fori_loop(t * ENT, (t + 1) * ENT, correct, 0, unroll=True)
            gap = (alpha - facts[t, 0, 2:3, :]) * sigma
            v = own[t].astype(F32)
            before[t] = v * sigma
            own[t] = ((local[t, 0, 0, :BD, :].astype(F32) - gap * v) * inverse).astype(BF)
            combine(t)
            finish(p, t, contract(t, 0, CH), one, beta, final)
            if t == 0:
                for u in range(BLK):
                    gather_sent(last, u)
            if not final:
                gather_first(p, t)
                gather_onward(p, t)
        return coefs

    def step(k, carry):
        return application(k, carry[0], carry[1], False), jnp.ones((1, BD), F32)

    coefs, sigma = lax.fori_loop(1, APPS - 1, step, (jnp.zeros((1, BD), F32), sigma0))
    coefs = application(APPS - 1, coefs, sigma, True)
    stats_send()
    stats_end()
    alpha = jnp.sum(jnp.sum(stats[...], axis=0), axis=0, keepdims=True) / count
    out_coef[...] = jnp.where(lane == 2 * APPS - 2, alpha, coefs)[:, :2 * APPS - 1]
    for t in range(BLK):
        out_vector[t] = own[t]
        out_rest[t] = leftover[t] - alpha * own[t].astype(F32)

    def sent(step, _):
        b = step // CHUNKS
        c = step % CHUNKS

        @pl.when(seg < segs - 1)
        def _():
            env_copy(0, b, c).wait_send()

        @pl.when(seg > 0)
        def _():
            env_copy(1, b, c).wait_send()

        return 0

    lax.fori_loop(0, BLK * CHUNKS, sent, 0)


def move(*refs):
    for i in range(3):
        refs[3 + i][...] = refs[i][...]


def hand_on(*arrays):
    hbm = pl.BlockSpec(memory_space=pltpu.VMEM)
    return pl.pallas_call(
        move,
        out_shape=tuple(jax.ShapeDtypeStruct(a.shape, a.dtype) for a in arrays),
        in_specs=[hbm] * 3,
        out_specs=(hbm,) * 3,
        name="hand_on",
    )(*arrays)


def on_device(segs, count, psi, env_left, env_right, site_left, site_right, mix_left, mix_right, sources, terms, term_coef, energy):
    vmem = pl.BlockSpec(memory_space=pltpu.VMEM)
    smem = pl.BlockSpec(memory_space=pltpu.SMEM)
    hbm = pl.BlockSpec(memory_space=pl.ANY)
    dma = pltpu.SemaphoreType.DMA
    vector, rest, coefs = pl.pallas_call(
        functools.partial(kernel, segs, count),
        out_shape=(
            jax.ShapeDtypeStruct((BLK, BD, BD), BF),
            jax.ShapeDtypeStruct((BLK, BD, BD), F32),
            jax.ShapeDtypeStruct((1, 2 * APPS - 1), F32),
        ),
        in_specs=[vmem, hbm, hbm, vmem, vmem, vmem, vmem, smem, smem, vmem, vmem],
        out_specs=(vmem, vmem, vmem),
        scratch_shapes=[
            pltpu.VMEM((2, BLK, CH, BD, BD), BF),
            pltpu.VMEM((2, BLK, CH, BD, BD), BF),
            pltpu.VMEM((2, BLK, CH, BD, BD), BF),
            pltpu.VMEM((CHUNK, BD, BD), BF),
            pltpu.VMEM((2, CH * TILE, 2 * CH * TILE), BF),
            pltpu.VMEM((2, 2, CH, CH), BF),
            pltpu.VMEM((2, BLK, BD, BD), BF),
            pltpu.VMEM((BD, CH * TILE), BF),
            pltpu.VMEM((CH * TILE, CH), BF),
            pltpu.VMEM((2, BLK, BD, BD), BF),
            pltpu.VMEM((BLK, CH * TILE, 2 * ENT * TILE), BF),
            pltpu.VMEM((BLK, CH, BD, BD), BF),
            pltpu.VMEM((BLK, BD, BD), F32),
            pltpu.VMEM((BLK, BD, BD), F32),
            pltpu.VMEM((BLK * ENT, BD, BD), BF),
            pltpu.VMEM((BLK, BD, BD), BF),
            pltpu.VMEM((BLK, BD, BD), F32),
            pltpu.VMEM((BLK, BD, BD), F32),
            pltpu.VMEM((2, BLK, 4, 4, ROWS, BD), BF),
            pltpu.VMEM((16, 8, BD), F32),
            pltpu.VMEM((BLK, 4, 4, ROWS, BD), BF),
            pltpu.VMEM((BLK, 16, 4, BD), F32),
            pltpu.SMEM((3, BLK * ENT), jnp.int32),
            dma((2, BLK + 1)),
            dma((2, BLK, CHUNKS)),
            dma((2, BLK, CHUNKS)),
            dma((2, BLK, 2, 2)),
            dma((2, BLK, 2, 2)),
            dma,
            dma,
        ],
        compiler_params=pltpu.CompilerParams(
            collective_id=0, has_side_effects=True, vmem_limit_bytes=56 * 2**20
        ),
        name="lanczos",
    )(
        psi[0], env_left[0], env_right[0], site_left[0], site_right[0], mix_left[0], mix_right[0],
        jnp.transpose(sources, (1, 0, 2)), jnp.transpose(terms, (1, 0, 2)), term_coef, jnp.transpose(energy, (1, 0, 2)),
    )
    vector, rest, coefs = hand_on(vector, rest, coefs)
    return vector[None], rest[None], coefs


def solution(mesh):
    in_specs = (
        P("seg", "sec", None, None),
        P("seg", "sec", None, None, None),
        P("seg", "sec", None, None, None),
        P("seg", "sec", None, None),
        P("seg", "sec", None, None),
        P("seg", None, None),
        P("seg", None, None),
        P("seg", "sec", None),
        P("seg", "sec", None),
        P(),
        P("seg", "sec", None),
    )
    out_specs = (P("seg", "sec", None, None), P("seg", "sec", None, None), P("seg", None))
    segs = mesh.shape["seg"]
    count = float(BLK * mesh.shape["sec"] * BD * BD)
    return jax.shard_map(
        functools.partial(on_device, segs, count), mesh=mesh, in_specs=in_specs, out_specs=out_specs, check_vma=False
    )
```

```python
import functools

import jax
import jax.numpy as jnp
from jax import lax
from jax.experimental import pallas as pl
from jax.experimental.pallas import tpu as pltpu
from jax.sharding import PartitionSpec as P

APPS = 6
EPSILON = 1e-06
CH = 40
BD = 128
ENT = 6
BLK = 3
HALF = BD // 2
TILE = 16
BY_ID = pl.DeviceIdType.LOGICAL
BF = jnp.bfloat16
F32 = jnp.float32

CHUNK = 8
CHUNKS = CH // CHUNK
LANES = BD // 2
ROWS = BD + TILE
PEERS = tuple((z, y) for z in range(4) for y in range(4) if (z, y) != (0, 0))


def dot(a, b):
    return lax.dot_general(a, b, (((1,), (0,)), ((), ())), preferred_element_type=F32)


def dot_nt(a, b):
    return lax.dot_general(a, b, (((1,), (1,)), ((), ())), preferred_element_type=F32)


def total(x):
    lanes = jnp.sum(x, axis=0, keepdims=True)
    return jnp.broadcast_to(jnp.sum(lanes, axis=1, keepdims=True), (1, BD))


def split(x):
    high = x.astype(BF)
    return high, (x - high.astype(F32)).astype(BF)


def wait_bytes(ref, sem):
    pltpu.make_async_copy(ref, ref, sem).wait()


def spread(rows, start):
    row = lax.broadcasted_iota(jnp.int32, (rows, CH), 0) + start
    return (row // TILE == lax.broadcasted_iota(jnp.int32, (rows, CH), 1)).astype(BF)


def same_state(rows, cols):
    row = lax.broadcasted_iota(jnp.int32, (rows, cols), 0)
    col = lax.broadcasted_iota(jnp.int32, (rows, cols), 1)
    return row % TILE == col % TILE


def kernel(
    segs,
    count,
    psi,
    env_left,
    env_right,
    site_left,
    site_right,
    mix_left,
    mix_right,
    sources,
    terms,
    term_coef,
    energy,
    out_vector,
    out_rest,
    out_coef,
    env_in,
    grown,
    envs,
    mixed,
    mix_kron,
    mix_parts,
    sites,
    pattern,
    chooser,
    site_t,
    term_kron,
    combo,
    image,
    on_site,
    picked,
    own,
    before,
    leftover,
    pieces,
    stats,
    local,
    facts,
    place,
    load_sem,
    env_send,
    env_recv,
    ssem,
    rsem,
    stat_send,
    stat_recv,
):
    seg = lax.axis_index("seg")
    sec = lax.axis_index("sec")
    my_z = sec // 4
    my_y = sec % 4

    def at(z, y):
        return seg * 16 + z * 4 + y

    to_z = {d: at((my_z + d) % 4, my_y) for d in (1, 2, 3)}
    to_y = {d: at(my_z, (my_y + d) % 4) for d in (1, 2, 3)}
    to_peer = {(dz, dy): at((my_z + dz) % 4, (my_y + dy) % 4) for dz, dy in PEERS}
    here = at(my_z, my_y)

    def send(src, dst, ssem, rsem, device):
        pltpu.make_async_remote_copy(
            src_ref=src, dst_ref=dst, send_sem=ssem, recv_sem=rsem,
            device_id=device, device_id_type=BY_ID,
        ).start()

    def load(side, b):
        ref = env_left if side == 0 else env_right
        return pltpu.make_async_copy(ref.at[b], env_in.at[side, b], load_sem.at[side, b])

    for side in range(2):
        load(side, 0).start()

    stats[0] = jnp.zeros((8, BD), F32)

    barrier = pltpu.get_barrier_semaphore()
    for dz, dy in PEERS:
        pl.semaphore_signal(barrier, inc=1, device_id=to_peer[dz, dy], device_id_type=BY_ID)

    @pl.when(seg > 0)
    def _():
        pl.semaphore_signal(barrier, inc=1, device_id=here - 16, device_id_type=BY_ID)

    @pl.when(seg < segs - 1)
    def _():
        pl.semaphore_signal(barrier, inc=1, device_id=here + 16, device_id_type=BY_ID)

    def end_copy(side):
        source = env_left if side == 0 else env_right
        return pltpu.make_async_copy(source, envs.at[side], load_sem.at[side, BLK])

    @pl.when(seg == 0)
    def _():
        end_copy(0).start()

    @pl.when(seg == segs - 1)
    def _():
        end_copy(1).start()

    pattern[...] = jnp.where(same_state(BD, CH * TILE), 1.0, 0.0).astype(BF)
    chooser[...] = spread(CH * TILE, 0)

    for side, (mix, site) in enumerate(((mix_left, site_left), (mix_right, site_right))):
        for part, value in enumerate(split(mix[...])):
            mix_parts[side, part] = value
        sites[side] = site[...]

    def spread_mix(side, rows):
        chosen = chooser[rows, :]
        for part in range(2):
            full = dot_nt(dot(chosen, mix_parts[side, part]).astype(BF), chooser[...])
            at = slice(part * CH * TILE, (part + 1) * CH * TILE)
            mix_kron[side, rows, at] = full.astype(BF) * pattern[...]

    eye_row = lax.broadcasted_iota(jnp.int32, (BD, BD), 0)
    eye = (eye_row == lax.broadcasted_iota(jnp.int32, (BD, BD), 1)).astype(BF)
    for side, ref in ((0, site_left), (1, site_right)):
        for b in range(BLK):
            site_t[side, b] = dot_nt(eye, ref[b]).astype(BF)

    for t in range(BLK):
        pieces[0, t, 0, 0, :BD, :] = psi[t]
        own[t] = psi[t]
    pieces[0, BLK - 1, 0, 0, BD:, :] = jnp.zeros((TILE, BD), BF)

    pl.semaphore_wait(
        barrier, len(PEERS) + jnp.where(seg > 0, 1, 0) + jnp.where(seg < segs - 1, 1, 0)
    )

    def height(t):
        return ROWS if t == BLK - 1 else BD

    def axes(t):
        return (0, to_y, pl.ds(0, HALF)), (1, to_z, pl.ds(HALF, height(t) - HALF))

    def direct(p, t, h):
        rows = pl.ds(0, height(t))
        return pieces.at[p, t, 0, pl.ds(1, 3), rows] if h == 0 else pieces.at[p, t, pl.ds(1, 3), 0, rows]

    def bundle(p, t, h, o, rows):
        return pieces.at[p, t, o, pl.ds(1, 3), rows] if h == 0 else pieces.at[p, t, pl.ds(1, 3), o, rows]

    def gather_first(p, t):
        rows = pl.ds(0, height(t))
        mine = pieces.at[p, t, 0, 0, rows]
        for d in (2, 1, 3):
            back = (4 - d) % 4
            send(mine, pieces.at[p, t, 0, back, rows], ssem.at[p, t, 0, 0], rsem.at[p, t, 0, 0], to_z[d])
            send(mine, pieces.at[p, t, back, 0, rows], ssem.at[p, t, 1, 0], rsem.at[p, t, 1, 0], to_y[d])

    def gather_second(p, t):
        for h, to, rows in axes(t):
            wait_bytes(direct(p, t, h), rsem.at[p, t, h, 0])
            for d in (2, 1, 3):
                back = (4 - d) % 4
                send(bundle(p, t, h, 0, rows), bundle(p, t, h, back, rows), ssem.at[p, t, h, 1], rsem.at[p, t, h, 1], to[d])

    def gather_end(p, t):
        for h, _, rows in axes(t):
            wait_bytes(pieces.at[p, t, pl.ds(1, 3), pl.ds(1, 3), rows], rsem.at[p, t, h, 1])
        local[t, :, :, :height(t), :] = pieces[p, t, :, :, :height(t), :]

    def gather_sent(p, t):
        for h, _, rows in axes(t):
            wait_bytes(direct(p, t, h), ssem.at[p, t, h, 0])
            wait_bytes(pieces.at[p, t, pl.ds(1, 3), pl.ds(1, 3), rows], ssem.at[p, t, h, 1])

    def gather_onward(p, t):
        if t > 0:
            gather_second(p, t - 1)
        if t == BLK - 1:
            gather_second(p, t)

    def stats_send():
        for dz, dy in PEERS:
            back = (4 - dy) % 4 * 4 + (4 - dz) % 4
            send(stats.at[0], stats.at[back], stat_send, stat_recv, to_peer[dz, dy])

    def stats_end():
        wait_bytes(stats.at[pl.ds(1, 15)], stat_recv)
        wait_bytes(stats.at[pl.ds(1, 15)], stat_send)

    def env_copy(side, b, c):
        part = pl.ds(c * CHUNK, CHUNK)
        to = here + 16 - 32 * side
        return pltpu.make_async_remote_copy(
            src_ref=grown.at[side, b, part],
            dst_ref=envs.at[side, b, part],
            send_sem=env_send.at[side, b, c],
            recv_sem=env_recv.at[side, b, c],
            device_id=to,
            device_id_type=BY_ID,
        )

    def grow(step, _):
        side = (step + 1 + seg) % 2
        b = step // 2 // CHUNKS
        c = step // 2 % CHUNKS
        rows = pl.ds(pl.multiple_of(c * CHUNK * TILE, CHUNK * TILE), CHUNK * TILE)

        @pl.when(c == 0)
        def _():
            wait_bytes(env_in.at[side, b], load_sem.at[side, b])

        @pl.when(b == 0)
        def _():
            spread_mix(side, rows)

        @pl.when(step == 1)
        def _():
            for late in range(1, BLK):
                load(0, late).start()
                load(1, late).start()

        maps = mix_kron[side, rows, :]
        for i in range(BD // (2 * TILE)):
            base = i * 2 * TILE
            cols = [
                env_in[side, b, :, base + h * TILE:base + (h + 1) * TILE, :].reshape(CH * TILE, BD)
                for h in range(2)
            ]
            both = jnp.concatenate(cols, axis=1)
            out = dot(maps, jnp.concatenate([both, both], axis=0)).astype(BF)
            for h in range(2):
                mixed[:, base + h * TILE:base + (h + 1) * TILE, :] = out[:, h * BD:(h + 1) * BD].reshape(
                    CHUNK, TILE, BD
                )
        half = dot(mixed[...].reshape(CHUNK * BD, BD), sites[side, b]).astype(BF)
        wide = jnp.concatenate([half[v * BD:(v + 1) * BD] for v in range(CHUNK)], axis=1)
        done = dot(site_t[side, b], wide).astype(BF)
        for v in range(CHUNK):
            grown[side, b, c * CHUNK + v] = done[:, v * BD:(v + 1) * BD]

        @pl.when(jnp.where(side == 0, seg < segs - 1, seg > 0))
        def _():
            env_copy(side, b, c).start()

        return 0

    lax.fori_loop(0, 2 * CHUNKS, grow, 0)
    for t in range(BLK):
        gather_first(0, t)
    lax.fori_loop(2 * CHUNKS, 4 * CHUNKS, grow, 0)
    for t in range(BLK):
        gather_second(0, t)
    lax.fori_loop(4 * CHUNKS, 6 * CHUNKS, grow, 0)

    for t in range(BLK):
        row = jnp.broadcast_to(energy[t], (BD, BD))
        on_site[t] = jnp.transpose(row)
    spread_all = spread(CH * TILE, 0)
    keep = same_state(CH * TILE, ENT * TILE)
    for t in range(BLK):
        entry = lax.broadcasted_iota(jnp.int32, (8, ENT * TILE), 1) // TILE
        kind = jnp.zeros((8, ENT * TILE), jnp.int32)
        for k in range(ENT):
            kind = jnp.where(entry == k, terms[t, 0, k], kind)
        hit = (kind == lax.broadcasted_iota(jnp.int32, (8, ENT * TILE), 0)).astype(BF)
        for part, coef in enumerate(split(term_coef[...])):
            rows = dot_nt(spread_all, coef).astype(BF)
            full = dot(rows, hit)
            term_kron[t, :, part * ENT * TILE:(part + 1) * ENT * TILE] = jnp.where(keep, full, 0.0).astype(BF)

    def where_is(t, k):
        s = sources[t, 0, k]
        owner = s // BLK
        sub = s - BLK * owner
        return sub, (owner % 4 - my_y + 4) % 4, (owner // 4 - my_z + 4) % 4

    for t in range(BLK):
        for k in range(ENT):
            for n, value in enumerate(where_is(t, k)):
                place[n, t * ENT + k] = value

    for t in range(BLK):
        gather_end(0, t)
        gather_sent(0, t)

    def fetch(q, _):
        sub, y, z = place[0, q], place[1, q], place[2, q]
        picked[q] = local[sub, y, z, :BD, :]
        return 0

    lax.fori_loop(0, BLK * ENT, fetch, 0)

    def squares(n, acc):
        t, o = n // 4, n % 4
        for i in range(4):
            x = local[t, o, i, :BD, :].astype(F32)
            acc = acc + x * x
        return acc

    norm = total(lax.fori_loop(0, BLK * 4, squares, jnp.zeros((BD, BD), F32)))
    sigma0 = 1.0 / jnp.sqrt(norm / count + EPSILON)

    lane = lax.broadcasted_iota(jnp.int32, (1, BD), 1)

    def combine(t):
        for i in range(BD // (2 * TILE)):
            base = i * 2 * TILE
            cols = [
                picked[t * ENT:(t + 1) * ENT, base + h * TILE:base + (h + 1) * TILE, :].reshape(ENT * TILE, BD)
                for h in range(2)
            ]
            both = jnp.concatenate(cols, axis=1)
            out = dot(term_kron[t], jnp.concatenate([both, both], axis=0)).astype(BF)
            for h in range(2):
                combo[t, :, base + h * TILE:base + (h + 1) * TILE, :] = out[:, h * BD:(h + 1) * BD].reshape(
                    CH, TILE, BD
                )

    def contract(t, first, n):
        inner = [dot(envs[0, t, first + j], combo[t, first + j]).astype(BF) for j in range(n)]
        right = [envs[1, t, first + j] for j in range(n)]
        return dot_nt(jnp.concatenate(inner, axis=1), jnp.concatenate(right, axis=1))

    def finish(p, t, applied, sigma, beta, final=False):
        v = own[t].astype(F32) * sigma
        img = applied * sigma + on_site[t] * v
        w = img if beta is None else img - beta * before[t]
        prod = total(img * v)
        norm = total(v * v)
        over = total(w * v)
        a = jnp.where(norm > 0.0, over / jnp.where(norm > 0.0, norm, 1.0), 0.0)
        y = w - a * v
        if final:
            leftover[t] = w
            stats[0, t:t + 1, :] = prod
            return None
        pieces[p, t, 0, 0, :BD, :] = y.astype(BF)
        return prod, norm, a, total(y * y)

    def tell(p, found):
        row = lax.broadcasted_iota(jnp.int32, (TILE, BD), 0)
        kind = row % 4
        pick = [jnp.where(lane < 32, x, jnp.where(lane < 64, y, z)) for x, y, z in zip(*found)]
        value = jnp.where(kind == 0, pick[0], jnp.where(kind == 1, pick[1], jnp.where(kind == 2, pick[2], pick[3])))
        one = value.astype(BF).astype(F32)
        two = (value - one).astype(BF).astype(F32)
        three = (value - one - two).astype(BF).astype(F32)
        tile = jnp.where(row < 4, one, jnp.where(row < 8, two, jnp.where(row < 12, three, 0.0)))
        pieces[p, BLK - 1, 0, 0, BD:, :] = tile.astype(BF)

    def learn():
        parts = local[BLK - 1, :, :, BD:, :].astype(F32).reshape(16, TILE, BD)
        value = parts[:, 0:4, :] + parts[:, 4:8, :] + parts[:, 8:12, :]
        for t in range(BLK):
            facts[t] = jnp.broadcast_to(value[:, :, 32 * t:32 * t + 1], (16, 4, BD))

    def scalars():
        alpha = jnp.zeros((1, BD), F32)
        for t in range(BLK):
            alpha = alpha + jnp.sum(facts[t], axis=0)[0:1, :]
        alpha = alpha / count
        squared = jnp.zeros((1, BD), F32)
        for t in range(BLK):
            gap = alpha - facts[t, :, 2, :]
            new = facts[t, :, 3, :] + gap * gap * facts[t, :, 1, :]
            squared = squared + jnp.sum(new, axis=0, keepdims=True)
        return alpha, jnp.sqrt(squared / count + EPSILON)

    for t in range(BLK):
        combine(t)

    @pl.when(seg == 0)
    def _():
        end_copy(0).wait()

    @pl.when(seg == segs - 1)
    def _():
        end_copy(1).wait()

    image[...] = jnp.zeros_like(image)

    found = []
    for b in range(BLK):
        def apply_first(c, _, b=b):
            @pl.when(seg > 0)
            def _():
                env_copy(0, b, c).wait_recv()

            @pl.when(seg < segs - 1)
            def _():
                env_copy(1, b, c).wait_recv()

            image[b] = image[b] + contract(b, c * CHUNK, CHUNK)
            return 0

        lax.fori_loop(0, CHUNKS, apply_first, 0)
        found.append(finish(1, b, image[b], sigma0, None))
        if b == BLK - 1:
            tell(1, found)
        gather_first(1, b)
        gather_onward(1, b)

    def application(k, coefs, sigma, final):
        last = k % 2
        p = (k + 1) % 2
        for t in range(BLK):
            gather_end(last, t)
            if t < BLK - 1:
                gather_sent(last, t)
        learn()
        alpha, beta = scalars()
        coefs = jnp.where(lane == 2 * k - 2, alpha, coefs)
        coefs = jnp.where(lane == 2 * k - 1, beta, coefs)
        inverse = 1.0 / beta

        def correct(q, _):
            sub, y, z = place[0, q], place[1, q], place[2, q]
            gap = (alpha - facts[sub, y * 4 + z, 2:3, :]) * sigma
            new = local[sub, y, z, :BD, :].astype(F32) - gap * picked[q].astype(F32)
            picked[q] = (new * inverse).astype(BF)
            return 0

        one = jnp.ones((1, BD), F32)
        found = []
        for t in range(BLK):
            lax.fori_loop(t * ENT, (t + 1) * ENT, correct, 0, unroll=True)
            gap = (alpha - facts[t, 0, 2:3, :]) * sigma
            v = own[t].astype(F32)
            before[t] = v * sigma
            own[t] = ((local[t, 0, 0, :BD, :].astype(F32) - gap * v) * inverse).astype(BF)
            combine(t)
            found.append(finish(p, t, contract(t, 0, CH), one, beta, final))
            if t == 0:
                gather_sent(last, BLK - 1)
            if not final:
                if t == BLK - 1:
                    tell(p, found)
                gather_first(p, t)
                gather_onward(p, t)
        return coefs

    def step(k, carry):
        return application(k, carry[0], carry[1], False), jnp.ones((1, BD), F32)

    coefs, sigma = lax.fori_loop(1, APPS - 1, step, (jnp.zeros((1, BD), F32), sigma0))
    coefs = application(APPS - 1, coefs, sigma, True)
    stats_send()
    stats_end()
    alpha = jnp.sum(jnp.sum(stats[...], axis=0), axis=0, keepdims=True) / count
    out_coef[...] = jnp.where(lane == 2 * APPS - 2, alpha, coefs)[:, :2 * APPS - 1]
    for t in range(BLK):
        out_vector[t] = own[t]
        out_rest[t] = leftover[t] - alpha * own[t].astype(F32)

    def sent(step, _):
        b = step // CHUNKS
        c = step % CHUNKS

        @pl.when(seg < segs - 1)
        def _():
            env_copy(0, b, c).wait_send()

        @pl.when(seg > 0)
        def _():
            env_copy(1, b, c).wait_send()

        return 0

    lax.fori_loop(0, BLK * CHUNKS, sent, 0)


def move(*refs):
    for i in range(3):
        refs[3 + i][...] = refs[i][...]


def hand_on(*arrays):
    hbm = pl.BlockSpec(memory_space=pltpu.VMEM)
    return pl.pallas_call(
        move,
        out_shape=tuple(jax.ShapeDtypeStruct(a.shape, a.dtype) for a in arrays),
        in_specs=[hbm] * 3,
        out_specs=(hbm,) * 3,
        name="hand_on",
    )(*arrays)


def on_device(segs, count, psi, env_left, env_right, site_left, site_right, mix_left, mix_right, sources, terms, term_coef, energy):
    vmem = pl.BlockSpec(memory_space=pltpu.VMEM)
    smem = pl.BlockSpec(memory_space=pltpu.SMEM)
    hbm = pl.BlockSpec(memory_space=pl.ANY)
    dma = pltpu.SemaphoreType.DMA
    vector, rest, coefs = pl.pallas_call(
        functools.partial(kernel, segs, count),
        out_shape=(
            jax.ShapeDtypeStruct((BLK, BD, BD), BF),
            jax.ShapeDtypeStruct((BLK, BD, BD), F32),
            jax.ShapeDtypeStruct((1, 2 * APPS - 1), F32),
        ),
        in_specs=[vmem, hbm, hbm, vmem, vmem, vmem, vmem, smem, smem, vmem, vmem],
        out_specs=(vmem, vmem, vmem),
        scratch_shapes=[
            pltpu.VMEM((2, BLK, CH, BD, BD), BF),
            pltpu.VMEM((2, BLK, CH, BD, BD), BF),
            pltpu.VMEM((2, BLK, CH, BD, BD), BF),
            pltpu.VMEM((CHUNK, BD, BD), BF),
            pltpu.VMEM((2, CH * TILE, 2 * CH * TILE), BF),
            pltpu.VMEM((2, 2, CH, CH), BF),
            pltpu.VMEM((2, BLK, BD, BD), BF),
            pltpu.VMEM((BD, CH * TILE), BF),
            pltpu.VMEM((CH * TILE, CH), BF),
            pltpu.VMEM((2, BLK, BD, BD), BF),
            pltpu.VMEM((BLK, CH * TILE, 2 * ENT * TILE), BF),
            pltpu.VMEM((BLK, CH, BD, BD), BF),
            pltpu.VMEM((BLK, BD, BD), F32),
            pltpu.VMEM((BLK, BD, BD), F32),
            pltpu.VMEM((BLK * ENT, BD, BD), BF),
            pltpu.VMEM((BLK, BD, BD), BF),
            pltpu.VMEM((BLK, BD, BD), F32),
            pltpu.VMEM((BLK, BD, BD), F32),
            pltpu.VMEM((2, BLK, 4, 4, ROWS, BD), BF),
            pltpu.VMEM((16, 8, BD), F32),
            pltpu.VMEM((BLK, 4, 4, ROWS, BD), BF),
            pltpu.VMEM((BLK, 16, 4, BD), F32),
            pltpu.SMEM((3, BLK * ENT), jnp.int32),
            dma((2, BLK + 1)),
            dma((2, BLK, CHUNKS)),
            dma((2, BLK, CHUNKS)),
            dma((2, BLK, 2, 2)),
            dma((2, BLK, 2, 2)),
            dma,
            dma,
        ],
        compiler_params=pltpu.CompilerParams(
            collective_id=0, has_side_effects=True, vmem_limit_bytes=56 * 2**20
        ),
        name="lanczos",
    )(
        psi[0], env_left[0], env_right[0], site_left[0], site_right[0], mix_left[0], mix_right[0],
        jnp.transpose(sources, (1, 0, 2)), jnp.transpose(terms, (1, 0, 2)), term_coef, jnp.transpose(energy, (1, 0, 2)),
    )
    vector, rest, coefs = hand_on(vector, rest, coefs)
    return vector[None], rest[None], coefs


def solution(mesh):
    in_specs = (
        P("seg", "sec", None, None),
        P("seg", "sec", None, None, None),
        P("seg", "sec", None, None, None),
        P("seg", "sec", None, None),
        P("seg", "sec", None, None),
        P("seg", None, None),
        P("seg", None, None),
        P("seg", "sec", None),
        P("seg", "sec", None),
        P(),
        P("seg", "sec", None),
    )
    out_specs = (P("seg", "sec", None, None), P("seg", "sec", None, None), P("seg", None))
    segs = mesh.shape["seg"]
    count = float(BLK * mesh.shape["sec"] * BD * BD)
    return jax.shard_map(
        functools.partial(on_device, segs, count), mesh=mesh, in_specs=in_specs, out_specs=out_specs, check_vma=False
    )
```

```python
import functools

import jax
import jax.numpy as jnp
from jax import lax
from jax.experimental import pallas as pl
from jax.experimental.pallas import tpu as pltpu
from jax.sharding import PartitionSpec as P

APPS = 6
EPSILON = 1e-06
CH = 40
BD = 128
ENT = 6
BLK = 3
HALF = BD // 2
TILE = 16
BY_ID = pl.DeviceIdType.LOGICAL
BF = jnp.bfloat16
F32 = jnp.float32

CHUNK = 8
CHUNKS = CH // CHUNK
LANES = BD // 2
ROWS = BD + TILE
PEERS = tuple((z, y) for z in range(4) for y in range(4) if (z, y) != (0, 0))


def dot(a, b):
    return lax.dot_general(a, b, (((1,), (0,)), ((), ())), preferred_element_type=F32)


def dot_nt(a, b):
    return lax.dot_general(a, b, (((1,), (1,)), ((), ())), preferred_element_type=F32)


def total(x):
    lanes = jnp.sum(x, axis=0, keepdims=True)
    return jnp.broadcast_to(jnp.sum(lanes, axis=1, keepdims=True), (1, BD))


def split(x):
    high = x.astype(BF)
    return high, (x - high.astype(F32)).astype(BF)


def wait_bytes(ref, sem):
    pltpu.make_async_copy(ref, ref, sem).wait()


def spread(rows, start):
    row = lax.broadcasted_iota(jnp.int32, (rows, CH), 0) + start
    return (row // TILE == lax.broadcasted_iota(jnp.int32, (rows, CH), 1)).astype(BF)


def same_state(rows, cols):
    row = lax.broadcasted_iota(jnp.int32, (rows, cols), 0)
    col = lax.broadcasted_iota(jnp.int32, (rows, cols), 1)
    return row % TILE == col % TILE


def kernel(
    segs,
    count,
    psi,
    env_left,
    env_right,
    site_left,
    site_right,
    mix_left,
    mix_right,
    sources,
    terms,
    term_coef,
    energy,
    out_vector,
    out_rest,
    out_coef,
    env_in,
    grown,
    envs,
    mixed,
    mix_kron,
    mix_parts,
    sites,
    pattern,
    chooser,
    site_t,
    term_kron,
    combo,
    image,
    on_site,
    picked,
    own,
    before,
    leftover,
    pieces,
    stats,
    local,
    facts,
    place,
    load_sem,
    env_send,
    env_recv,
    ssem,
    rsem,
    stat_send,
    stat_recv,
):
    seg = lax.axis_index("seg")
    sec = lax.axis_index("sec")
    my_z = sec // 4
    my_y = sec % 4

    def at(z, y):
        return seg * 16 + z * 4 + y

    to_z = {d: at((my_z + d) % 4, my_y) for d in (1, 2, 3)}
    to_y = {d: at(my_z, (my_y + d) % 4) for d in (1, 2, 3)}
    to_peer = {(dz, dy): at((my_z + dz) % 4, (my_y + dy) % 4) for dz, dy in PEERS}
    here = at(my_z, my_y)

    def send(src, dst, ssem, rsem, device):
        pltpu.make_async_remote_copy(
            src_ref=src, dst_ref=dst, send_sem=ssem, recv_sem=rsem,
            device_id=device, device_id_type=BY_ID,
        ).start()

    def load(side, b):
        ref = env_left if side == 0 else env_right
        return pltpu.make_async_copy(ref.at[b], env_in.at[side, b], load_sem.at[side, b])

    for side in range(2):
        load(side, 0).start()

    stats[0] = jnp.zeros((8, BD), F32)

    barrier = pltpu.get_barrier_semaphore()
    for dz, dy in PEERS:
        pl.semaphore_signal(barrier, inc=1, device_id=to_peer[dz, dy], device_id_type=BY_ID)

    @pl.when(seg > 0)
    def _():
        pl.semaphore_signal(barrier, inc=1, device_id=here - 16, device_id_type=BY_ID)

    @pl.when(seg < segs - 1)
    def _():
        pl.semaphore_signal(barrier, inc=1, device_id=here + 16, device_id_type=BY_ID)

    def end_copy(side):
        source = env_left if side == 0 else env_right
        return pltpu.make_async_copy(source, envs.at[side], load_sem.at[side, BLK])

    @pl.when(seg == 0)
    def _():
        end_copy(0).start()

    @pl.when(seg == segs - 1)
    def _():
        end_copy(1).start()

    pattern[...] = jnp.where(same_state(BD, CH * TILE), 1.0, 0.0).astype(BF)
    chooser[...] = spread(CH * TILE, 0)

    for side, (mix, site) in enumerate(((mix_left, site_left), (mix_right, site_right))):
        for part, value in enumerate(split(mix[...])):
            mix_parts[side, part] = value
        sites[side] = site[...]

    def spread_mix(side, rows):
        chosen = chooser[rows, :]
        for part in range(2):
            full = dot_nt(dot(chosen, mix_parts[side, part]).astype(BF), chooser[...])
            at = slice(part * CH * TILE, (part + 1) * CH * TILE)
            mix_kron[side, rows, at] = full.astype(BF) * pattern[...]

    eye_row = lax.broadcasted_iota(jnp.int32, (BD, BD), 0)
    eye = (eye_row == lax.broadcasted_iota(jnp.int32, (BD, BD), 1)).astype(BF)
    for side, ref in ((0, site_left), (1, site_right)):
        for b in range(BLK):
            site_t[side, b] = dot_nt(eye, ref[b]).astype(BF)

    for t in range(BLK):
        pieces[0, t, 0, 0, :BD, :] = psi[t]
        own[t] = psi[t]
    pieces[0, BLK - 1, 0, 0, BD:, :] = jnp.zeros((TILE, BD), BF)

    pl.semaphore_wait(
        barrier, len(PEERS) + jnp.where(seg > 0, 1, 0) + jnp.where(seg < segs - 1, 1, 0)
    )

    def height(t):
        return ROWS if t == BLK - 1 else BD

    def axes(t):
        return (0, to_y, pl.ds(0, HALF)), (1, to_z, pl.ds(HALF, height(t) - HALF))

    def direct(p, t, h):
        rows = pl.ds(0, height(t))
        return pieces.at[p, t, 0, pl.ds(1, 3), rows] if h == 0 else pieces.at[p, t, pl.ds(1, 3), 0, rows]

    def bundle(p, t, h, o, rows):
        return pieces.at[p, t, o, pl.ds(1, 3), rows] if h == 0 else pieces.at[p, t, pl.ds(1, 3), o, rows]

    def gather_first(p, t):
        rows = pl.ds(0, height(t))
        mine = pieces.at[p, t, 0, 0, rows]
        for d in (2, 1, 3):
            back = (4 - d) % 4
            send(mine, pieces.at[p, t, 0, back, rows], ssem.at[p, t, 0, 0], rsem.at[p, t, 0, 0], to_z[d])
            send(mine, pieces.at[p, t, back, 0, rows], ssem.at[p, t, 1, 0], rsem.at[p, t, 1, 0], to_y[d])

    def both(p, h, o, rows):
        ts = pl.ds(0, 2)
        return pieces.at[p, ts, o, pl.ds(1, 3), rows] if h == 0 else pieces.at[p, ts, pl.ds(1, 3), o, rows]

    def gather_second(p, t):
        if t == 0:
            return
        if t == 1:
            for h, to, rows in axes(t):
                wait_bytes(direct(p, 0, h), rsem.at[p, 0, h, 0])
                wait_bytes(direct(p, 1, h), rsem.at[p, 1, h, 0])
                for d in (2, 1, 3):
                    back = (4 - d) % 4
                    send(both(p, h, 0, rows), both(p, h, back, rows), ssem.at[p, t, h, 1], rsem.at[p, t, h, 1], to[d])
            return
        for h, to, rows in axes(t):
            wait_bytes(direct(p, t, h), rsem.at[p, t, h, 0])
            for d in (2, 1, 3):
                back = (4 - d) % 4
                send(bundle(p, t, h, 0, rows), bundle(p, t, h, back, rows), ssem.at[p, t, h, 1], rsem.at[p, t, h, 1], to[d])

    def gather_end(p, t):
        for h, _, rows in axes(t):
            if t == 0:
                wait_bytes(pieces.at[p, pl.ds(0, 2), pl.ds(1, 3), pl.ds(1, 3), rows], rsem.at[p, 1, h, 1])
            if t == 2:
                wait_bytes(pieces.at[p, t, pl.ds(1, 3), pl.ds(1, 3), rows], rsem.at[p, t, h, 1])
        local[t, :, :, :height(t), :] = pieces[p, t, :, :, :height(t), :]

    def gather_sent(p, t):
        for h, _, rows in axes(t):
            wait_bytes(direct(p, t, h), ssem.at[p, t, h, 0])
            if t == 0:
                wait_bytes(pieces.at[p, pl.ds(0, 2), pl.ds(1, 3), pl.ds(1, 3), rows], ssem.at[p, 1, h, 1])
            if t == 2:
                wait_bytes(pieces.at[p, t, pl.ds(1, 3), pl.ds(1, 3), rows], ssem.at[p, t, h, 1])

    def gather_onward(p, t):
        if t > 0:
            gather_second(p, t - 1)
        if t == BLK - 1:
            gather_second(p, t)

    def stats_send():
        for dz, dy in PEERS:
            back = (4 - dy) % 4 * 4 + (4 - dz) % 4
            send(stats.at[0], stats.at[back], stat_send, stat_recv, to_peer[dz, dy])

    def stats_end():
        wait_bytes(stats.at[pl.ds(1, 15)], stat_recv)
        wait_bytes(stats.at[pl.ds(1, 15)], stat_send)

    def env_copy(side, b, c):
        part = pl.ds(c * CHUNK, CHUNK)
        to = here + 16 - 32 * side
        return pltpu.make_async_remote_copy(
            src_ref=grown.at[side, b, part],
            dst_ref=envs.at[side, b, part],
            send_sem=env_send.at[side, b, c],
            recv_sem=env_recv.at[side, b, c],
            device_id=to,
            device_id_type=BY_ID,
        )

    def grow(step, _):
        side = (step + 1 + seg) % 2
        b = step // 2 // CHUNKS
        c = step // 2 % CHUNKS
        rows = pl.ds(pl.multiple_of(c * CHUNK * TILE, CHUNK * TILE), CHUNK * TILE)

        @pl.when(c == 0)
        def _():
            wait_bytes(env_in.at[side, b], load_sem.at[side, b])

        @pl.when(b == 0)
        def _():
            spread_mix(side, rows)

        @pl.when(step == 1)
        def _():
            for late in range(1, BLK):
                load(0, late).start()
                load(1, late).start()

        maps = mix_kron[side, rows, :]
        for i in range(BD // (2 * TILE)):
            base = i * 2 * TILE
            cols = [
                env_in[side, b, :, base + h * TILE:base + (h + 1) * TILE, :].reshape(CH * TILE, BD)
                for h in range(2)
            ]
            both = jnp.concatenate(cols, axis=1)
            out = dot(maps, jnp.concatenate([both, both], axis=0)).astype(BF)
            for h in range(2):
                mixed[:, base + h * TILE:base + (h + 1) * TILE, :] = out[:, h * BD:(h + 1) * BD].reshape(
                    CHUNK, TILE, BD
                )
        half = dot(mixed[...].reshape(CHUNK * BD, BD), sites[side, b]).astype(BF)
        wide = jnp.concatenate([half[v * BD:(v + 1) * BD] for v in range(CHUNK)], axis=1)
        done = dot(site_t[side, b], wide).astype(BF)
        for v in range(CHUNK):
            grown[side, b, c * CHUNK + v] = done[:, v * BD:(v + 1) * BD]

        @pl.when(jnp.where(side == 0, seg < segs - 1, seg > 0))
        def _():
            env_copy(side, b, c).start()

        return 0

    lax.fori_loop(0, 2 * CHUNKS, grow, 0)
    for t in range(BLK):
        gather_first(0, t)
    lax.fori_loop(2 * CHUNKS, 4 * CHUNKS, grow, 0)
    for t in range(BLK):
        gather_second(0, t)
    lax.fori_loop(4 * CHUNKS, 6 * CHUNKS, grow, 0)

    for t in range(BLK):
        row = jnp.broadcast_to(energy[t], (BD, BD))
        on_site[t] = jnp.transpose(row)
    spread_all = spread(CH * TILE, 0)
    keep = same_state(CH * TILE, ENT * TILE)
    for t in range(BLK):
        entry = lax.broadcasted_iota(jnp.int32, (8, ENT * TILE), 1) // TILE
        kind = jnp.zeros((8, ENT * TILE), jnp.int32)
        for k in range(ENT):
            kind = jnp.where(entry == k, terms[t, 0, k], kind)
        hit = (kind == lax.broadcasted_iota(jnp.int32, (8, ENT * TILE), 0)).astype(BF)
        for part, coef in enumerate(split(term_coef[...])):
            rows = dot_nt(spread_all, coef).astype(BF)
            full = dot(rows, hit)
            term_kron[t, :, part * ENT * TILE:(part + 1) * ENT * TILE] = jnp.where(keep, full, 0.0).astype(BF)

    def where_is(t, k):
        s = sources[t, 0, k]
        owner = s // BLK
        sub = s - BLK * owner
        return sub, (owner % 4 - my_y + 4) % 4, (owner // 4 - my_z + 4) % 4

    for t in range(BLK):
        for k in range(ENT):
            for n, value in enumerate(where_is(t, k)):
                place[n, t * ENT + k] = value

    for t in range(BLK):
        gather_end(0, t)
        gather_sent(0, t)

    def fetch(q, _):
        sub, y, z = place[0, q], place[1, q], place[2, q]
        picked[q] = local[sub, y, z, :BD, :]
        return 0

    lax.fori_loop(0, BLK * ENT, fetch, 0)

    def squares(n, acc):
        t, o = n // 4, n % 4
        for i in range(4):
            x = local[t, o, i, :BD, :].astype(F32)
            acc = acc + x * x
        return acc

    norm = total(lax.fori_loop(0, BLK * 4, squares, jnp.zeros((BD, BD), F32)))
    sigma0 = 1.0 / jnp.sqrt(norm / count + EPSILON)

    lane = lax.broadcasted_iota(jnp.int32, (1, BD), 1)

    def combine(t):
        for i in range(BD // (2 * TILE)):
            base = i * 2 * TILE
            cols = [
                picked[t * ENT:(t + 1) * ENT, base + h * TILE:base + (h + 1) * TILE, :].reshape(ENT * TILE, BD)
                for h in range(2)
            ]
            both = jnp.concatenate(cols, axis=1)
            out = dot(term_kron[t], jnp.concatenate([both, both], axis=0)).astype(BF)
            for h in range(2):
                combo[t, :, base + h * TILE:base + (h + 1) * TILE, :] = out[:, h * BD:(h + 1) * BD].reshape(
                    CH, TILE, BD
                )

    def contract(t, first, n):
        inner = [dot(envs[0, t, first + j], combo[t, first + j]).astype(BF) for j in range(n)]
        right = [envs[1, t, first + j] for j in range(n)]
        return dot_nt(jnp.concatenate(inner, axis=1), jnp.concatenate(right, axis=1))

    def finish(p, t, applied, sigma, beta, final=False):
        v = own[t].astype(F32) * sigma
        img = applied * sigma + on_site[t] * v
        w = img if beta is None else img - beta * before[t]
        prod = total(img * v)
        norm = total(v * v)
        over = total(w * v)
        a = jnp.where(norm > 0.0, over / jnp.where(norm > 0.0, norm, 1.0), 0.0)
        y = w - a * v
        if final:
            leftover[t] = w
            stats[0, t:t + 1, :] = prod
            return None
        pieces[p, t, 0, 0, :BD, :] = y.astype(BF)
        return prod, norm, a, total(y * y)

    def tell(p, found):
        row = lax.broadcasted_iota(jnp.int32, (TILE, BD), 0)
        kind = row % 4
        pick = [jnp.where(lane < 32, x, jnp.where(lane < 64, y, z)) for x, y, z in zip(*found)]
        value = jnp.where(kind == 0, pick[0], jnp.where(kind == 1, pick[1], jnp.where(kind == 2, pick[2], pick[3])))
        one = value.astype(BF).astype(F32)
        two = (value - one).astype(BF).astype(F32)
        three = (value - one - two).astype(BF).astype(F32)
        tile = jnp.where(row < 4, one, jnp.where(row < 8, two, jnp.where(row < 12, three, 0.0)))
        pieces[p, BLK - 1, 0, 0, BD:, :] = tile.astype(BF)

    def learn():
        parts = local[BLK - 1, :, :, BD:, :].astype(F32).reshape(16, TILE, BD)
        value = parts[:, 0:4, :] + parts[:, 4:8, :] + parts[:, 8:12, :]
        for t in range(BLK):
            facts[t] = jnp.broadcast_to(value[:, :, 32 * t:32 * t + 1], (16, 4, BD))

    def scalars():
        alpha = jnp.zeros((1, BD), F32)
        for t in range(BLK):
            alpha = alpha + jnp.sum(facts[t], axis=0)[0:1, :]
        alpha = alpha / count
        squared = jnp.zeros((1, BD), F32)
        for t in range(BLK):
            gap = alpha - facts[t, :, 2, :]
            new = facts[t, :, 3, :] + gap * gap * facts[t, :, 1, :]
            squared = squared + jnp.sum(new, axis=0, keepdims=True)
        return alpha, jnp.sqrt(squared / count + EPSILON)

    for t in range(BLK):
        combine(t)

    @pl.when(seg == 0)
    def _():
        end_copy(0).wait()

    @pl.when(seg == segs - 1)
    def _():
        end_copy(1).wait()

    image[...] = jnp.zeros_like(image)

    found = []
    for b in range(BLK):
        def apply_first(c, _, b=b):
            @pl.when(seg > 0)
            def _():
                env_copy(0, b, c).wait_recv()

            @pl.when(seg < segs - 1)
            def _():
                env_copy(1, b, c).wait_recv()

            image[b] = image[b] + contract(b, c * CHUNK, CHUNK)
            return 0

        lax.fori_loop(0, CHUNKS, apply_first, 0)
        found.append(finish(1, b, image[b], sigma0, None))
        if b == BLK - 1:
            tell(1, found)
        gather_first(1, b)
        gather_onward(1, b)

    def application(k, coefs, sigma, final):
        last = k % 2
        p = (k + 1) % 2
        for t in range(BLK):
            gather_end(last, t)
            if t < BLK - 1:
                gather_sent(last, t)
        learn()
        alpha, beta = scalars()
        coefs = jnp.where(lane == 2 * k - 2, alpha, coefs)
        coefs = jnp.where(lane == 2 * k - 1, beta, coefs)
        inverse = 1.0 / beta

        def correct(q, _):
            sub, y, z = place[0, q], place[1, q], place[2, q]
            gap = (alpha - facts[sub, y * 4 + z, 2:3, :]) * sigma
            new = local[sub, y, z, :BD, :].astype(F32) - gap * picked[q].astype(F32)
            picked[q] = (new * inverse).astype(BF)
            return 0

        one = jnp.ones((1, BD), F32)
        found = []
        for t in range(BLK):
            lax.fori_loop(t * ENT, (t + 1) * ENT, correct, 0, unroll=True)
            gap = (alpha - facts[t, 0, 2:3, :]) * sigma
            v = own[t].astype(F32)
            before[t] = v * sigma
            own[t] = ((local[t, 0, 0, :BD, :].astype(F32) - gap * v) * inverse).astype(BF)
            combine(t)
            found.append(finish(p, t, contract(t, 0, CH), one, beta, final))
            if t == 0:
                gather_sent(last, BLK - 1)
            if not final:
                if t == BLK - 1:
                    tell(p, found)
                gather_first(p, t)
                gather_onward(p, t)
        return coefs

    def step(k, carry):
        return application(k, carry[0], carry[1], False), jnp.ones((1, BD), F32)

    coefs, sigma = lax.fori_loop(1, APPS - 1, step, (jnp.zeros((1, BD), F32), sigma0))
    coefs = application(APPS - 1, coefs, sigma, True)
    stats_send()
    stats_end()
    alpha = jnp.sum(jnp.sum(stats[...], axis=0), axis=0, keepdims=True) / count
    out_coef[...] = jnp.where(lane == 2 * APPS - 2, alpha, coefs)[:, :2 * APPS - 1]
    for t in range(BLK):
        out_vector[t] = own[t]
        out_rest[t] = leftover[t] - alpha * own[t].astype(F32)

    def sent(step, _):
        b = step // CHUNKS
        c = step % CHUNKS

        @pl.when(seg < segs - 1)
        def _():
            env_copy(0, b, c).wait_send()

        @pl.when(seg > 0)
        def _():
            env_copy(1, b, c).wait_send()

        return 0

    lax.fori_loop(0, BLK * CHUNKS, sent, 0)


def move(*refs):
    for i in range(3):
        refs[3 + i][...] = refs[i][...]


def hand_on(*arrays):
    hbm = pl.BlockSpec(memory_space=pltpu.VMEM)
    return pl.pallas_call(
        move,
        out_shape=tuple(jax.ShapeDtypeStruct(a.shape, a.dtype) for a in arrays),
        in_specs=[hbm] * 3,
        out_specs=(hbm,) * 3,
        name="hand_on",
    )(*arrays)


def on_device(segs, count, psi, env_left, env_right, site_left, site_right, mix_left, mix_right, sources, terms, term_coef, energy):
    vmem = pl.BlockSpec(memory_space=pltpu.VMEM)
    smem = pl.BlockSpec(memory_space=pltpu.SMEM)
    hbm = pl.BlockSpec(memory_space=pl.ANY)
    dma = pltpu.SemaphoreType.DMA
    vector, rest, coefs = pl.pallas_call(
        functools.partial(kernel, segs, count),
        out_shape=(
            jax.ShapeDtypeStruct((BLK, BD, BD), BF),
            jax.ShapeDtypeStruct((BLK, BD, BD), F32),
            jax.ShapeDtypeStruct((1, 2 * APPS - 1), F32),
        ),
        in_specs=[vmem, hbm, hbm, vmem, vmem, vmem, vmem, smem, smem, vmem, vmem],
        out_specs=(vmem, vmem, vmem),
        scratch_shapes=[
            pltpu.VMEM((2, BLK, CH, BD, BD), BF),
            pltpu.VMEM((2, BLK, CH, BD, BD), BF),
            pltpu.VMEM((2, BLK, CH, BD, BD), BF),
            pltpu.VMEM((CHUNK, BD, BD), BF),
            pltpu.VMEM((2, CH * TILE, 2 * CH * TILE), BF),
            pltpu.VMEM((2, 2, CH, CH), BF),
            pltpu.VMEM((2, BLK, BD, BD), BF),
            pltpu.VMEM((BD, CH * TILE), BF),
            pltpu.VMEM((CH * TILE, CH), BF),
            pltpu.VMEM((2, BLK, BD, BD), BF),
            pltpu.VMEM((BLK, CH * TILE, 2 * ENT * TILE), BF),
            pltpu.VMEM((BLK, CH, BD, BD), BF),
            pltpu.VMEM((BLK, BD, BD), F32),
            pltpu.VMEM((BLK, BD, BD), F32),
            pltpu.VMEM((BLK * ENT, BD, BD), BF),
            pltpu.VMEM((BLK, BD, BD), BF),
            pltpu.VMEM((BLK, BD, BD), F32),
            pltpu.VMEM((BLK, BD, BD), F32),
            pltpu.VMEM((2, BLK, 4, 4, ROWS, BD), BF),
            pltpu.VMEM((16, 8, BD), F32),
            pltpu.VMEM((BLK, 4, 4, ROWS, BD), BF),
            pltpu.VMEM((BLK, 16, 4, BD), F32),
            pltpu.SMEM((3, BLK * ENT), jnp.int32),
            dma((2, BLK + 1)),
            dma((2, BLK, CHUNKS)),
            dma((2, BLK, CHUNKS)),
            dma((2, BLK, 2, 2)),
            dma((2, BLK, 2, 2)),
            dma,
            dma,
        ],
        compiler_params=pltpu.CompilerParams(
            collective_id=0, has_side_effects=True, vmem_limit_bytes=56 * 2**20
        ),
        name="lanczos",
    )(
        psi[0], env_left[0], env_right[0], site_left[0], site_right[0], mix_left[0], mix_right[0],
        jnp.transpose(sources, (1, 0, 2)), jnp.transpose(terms, (1, 0, 2)), term_coef, jnp.transpose(energy, (1, 0, 2)),
    )
    vector, rest, coefs = hand_on(vector, rest, coefs)
    return vector[None], rest[None], coefs


def solution(mesh):
    in_specs = (
        P("seg", "sec", None, None),
        P("seg", "sec", None, None, None),
        P("seg", "sec", None, None, None),
        P("seg", "sec", None, None),
        P("seg", "sec", None, None),
        P("seg", None, None),
        P("seg", None, None),
        P("seg", "sec", None),
        P("seg", "sec", None),
        P(),
        P("seg", "sec", None),
    )
    out_specs = (P("seg", "sec", None, None), P("seg", "sec", None, None), P("seg", None))
    segs = mesh.shape["seg"]
    count = float(BLK * mesh.shape["sec"] * BD * BD)
    return jax.shard_map(
        functools.partial(on_device, segs, count), mesh=mesh, in_specs=in_specs, out_specs=out_specs, check_vma=False
    )
```
